256 devices in a mesh: dp: 16 (over z, y_hi), fsdp: 16 (over y_lo, x, core).
Axes of the slice: x: 4, y: 4 (y_hi: 2, y_lo: 2; y = y_hi * 2 + y_lo), z: 8, core: 2. Of those that a mesh axis runs over, the one named last changes fastest.
Arguments:
- hidden_input: bfloat16 [2048, 32, 8192], P(('dp', 'fsdp')), may hold values from -6 to 6
- input_norm_gain: float32 [8192], replicated, may hold values from 0.8 to 3
- joined_weight: bfloat16 [8192, 768], P('fsdp'), may hold values from -0.0625 to 0.0625
- joined_bias: bfloat16 [768], replicated, may hold values from -3 to 3
- adapter_down: bfloat16 [8192, 64], replicated, may hold values from -0.0625 to 0.0625
- adapter_up: bfloat16 [64, 512], replicated, may hold values from -0.75 to 0.75
- advantage: float32 [2048], P(('dp', 'fsdp')), may hold values from -4 to 4
- output_gradient: bfloat16 [2048, 32, 512], P(('dp', 'fsdp')), may hold values from -6 to 6
- lengths: int32 [2048], P(('dp', 'fsdp')), may hold values from 1 to 32, as said below
- assignment: int32 [2048], P(('dp', 'fsdp')), may hold values from 0 to 15, as said below
Outputs:
- att_out: bfloat16 [2048, 32, 512], P(('dp', 'fsdp'))
- down_gradient: float32 [8192, 64], P('dp')
- up_gradient: float32 [64, 512], P(None, 'dp')
The draws below stay inside these ranges and needn't reach their ends.
Inputs may be any that keep to these rules, and one draw needn't show every extreme that they name: `assignment`: among the rollouts of the devices that share one fsdp index, every dp index is named by exactly 8 of them, and the 8 rollouts of one device name different dp indices. `lengths`: every device holds a rollout of length 32.
All inputs are finite; a program needn't handle non-finite values.
Results may differ from the reference program's by a relative error of at most 0.02.
The reference program's roundings to bfloat16 on the way count: a program that leaves them out, or rounds other values in their place, can miss the bound.
Values may be sent and summed in bfloat16 or wider, within the bound.
A program may use at most 128 MiB of HBM per device.

```python
import jax
import jax.numpy as jnp
from jax import lax

MODEL_WIDTH_DIM = 8192
HEAD_WIDTH = 128
QUERY_HEADS = 4
ADAPTER_RANK = 64
L = 32
ROLL_DEV = 8
ROLLOUTS = 2048
N_DP = 16
N_FSDP = 16


def draw_input_norm_gain(key, part):
    key = jax.random.fold_in(key, 37)
    return jax.random.uniform(key, (MODEL_WIDTH_DIM,), jnp.float32, 0.8, 1.25)


def draw_lengths(key, part):
    key = jax.random.fold_in(key, 11)
    key_base, key_pick = jax.random.split(key)
    base_len = jax.random.randint(key_base, (ROLLOUTS,), 1, L + 1)
    longest = jax.random.randint(key_pick, (ROLLOUTS // ROLL_DEV,), 0, ROLL_DEV)
    rollout_index = jnp.arange(ROLLOUTS)
    device_slot = rollout_index % ROLL_DEV
    device_index = rollout_index // ROLL_DEV
    return jnp.where(device_slot == longest[device_index], L, base_len).astype(jnp.int32)


def column_plan(key):
    key_dest, key_src, key_shift, key_order = jax.random.split(key, 4)
    dest_perm = jax.random.permutation(key_dest, N_DP)
    source_offset = jax.random.permutation(key_src, N_DP)
    shifts = jax.random.permutation(key_shift, N_DP)[:ROLL_DEV]
    orders = jax.vmap(lambda key_one: jax.random.permutation(key_one, ROLL_DEV))(jax.random.split(key_order, N_DP))
    position = (source_offset[:, None] + shifts[orders]) % N_DP
    return dest_perm[position]


def draw_assignment(key, part):
    key = jax.random.fold_in(key, 23)
    columns = jax.vmap(column_plan)(jax.random.split(key, N_FSDP))
    return jnp.transpose(columns, (1, 0, 2)).reshape(ROLLOUTS).astype(jnp.int32)


def block_levels(key, shape, cuts, smallest, top_value):
    def one(axis_at, parts):
        draws = jax.random.uniform(jax.random.fold_in(jax.random.fold_in(key, 6), axis_at), (parts,), jnp.float32, smallest / len(cuts), top_value / len(cuts))
        return jnp.repeat(jnp.exp(draws), shape[axis_at] // parts).reshape((-1,) + (1,) * (len(shape) - axis_at - 1))

    factor_of = one(*cuts[0])
    for cut in cuts[1:]:
        factor_of = factor_of * one(*cut)
    return factor_of


def gaussian(rng, extent, scale, bound, pieces=(), held_as=jnp.bfloat16):
    values = scale * jax.random.normal(rng, extent, jnp.float32)
    if pieces:
        values = values * block_levels(rng, extent, pieces, -0.22, 0.18)
    return jnp.clip(values, -bound, bound).astype(held_as)


def setup_inputs(seed: int = 0) -> dict:
    keys = jax.random.split(jax.random.key(seed), 11)
    hidden_input = gaussian(keys[0], (ROLLOUTS, L, MODEL_WIDTH_DIM), 1.0, 6.0, ((0, 256),))
    input_norm_gain = draw_input_norm_gain(jax.random.fold_in(keys[10], 71), 0)
    joined_weight = gaussian(keys[2], (MODEL_WIDTH_DIM, QUERY_HEADS * HEAD_WIDTH + 2 * HEAD_WIDTH), MODEL_WIDTH_DIM ** -0.5, 0.0625, ((0, 16),))
    joined_bias = gaussian(keys[3], (QUERY_HEADS * HEAD_WIDTH + 2 * HEAD_WIDTH,), 0.5, 3.0)
    adapter_down = gaussian(keys[4], (MODEL_WIDTH_DIM, ADAPTER_RANK), MODEL_WIDTH_DIM ** -0.5, 0.0625)
    adapter_up = gaussian(keys[5], (ADAPTER_RANK, QUERY_HEADS * HEAD_WIDTH), ADAPTER_RANK ** -0.5, 0.75)
    advantage = gaussian(keys[6], (ROLLOUTS,), 1.0, 4.0, ((0, 256),), jnp.float32)
    output_gradient = gaussian(keys[7], (ROLLOUTS, L, QUERY_HEADS * HEAD_WIDTH), 1.0, 6.0, ((0, 256),))
    lengths = draw_lengths(jax.random.fold_in(keys[10], 71), 0)
    assignment = draw_assignment(jax.random.fold_in(keys[10], 71), 0)
    return {"hidden_input": hidden_input, "input_norm_gain": input_norm_gain, "joined_weight": joined_weight, "joined_bias": joined_bias, "adapter_down": adapter_down, "adapter_up": adapter_up, "advantage": advantage, "output_gradient": output_gradient, "lengths": lengths, "assignment": assignment}


EPSILON = 1e-06
ADAPTER_SCALE = 2.0

def normalize(hidden_rows, gain):
    hidden_wide = hidden_rows.astype(jnp.float32)
    scale_rows = lax.rsqrt(lax.optimization_barrier(jnp.mean(hidden_wide * hidden_wide, axis=-1, keepdims=True)) + EPSILON)
    return (hidden_wide * scale_rows * gain.astype(jnp.float32)).astype(jnp.bfloat16)

def weigh_grad(gradient_rows, adv_rows, length_rows):
    factor = adv_rows.astype(jnp.float32) / length_rows.astype(jnp.float32)
    return (gradient_rows.astype(jnp.float32) * factor[:, None, None]).astype(jnp.bfloat16)

def attention(query_rows, keys_rows, values_rows, input_lengths):
    rollouts_here = input_lengths.shape[0]
    slot_len = query_rows.shape[0] // rollouts_here
    head_size = keys_rows.shape[1]
    num_heads = query_rows.shape[1] // head_size
    query_four = query_rows.reshape(rollouts_here, slot_len, num_heads, head_size).astype(jnp.float32)
    key_three = keys_rows.reshape(rollouts_here, slot_len, head_size).astype(jnp.float32)
    value_three = values_rows.reshape(rollouts_here, slot_len, head_size).astype(jnp.float32)
    scores = jnp.einsum('rqhd,rkd->rhqk', query_four, key_three) * head_size ** (-0.5)
    position = jnp.arange(slot_len, dtype=jnp.int32)
    visible = (position[None, None, None, :] <= position[None, None, :, None]) & (position[None, None, None, :] < input_lengths[:, None, None, None])
    scores = jnp.where(visible, scores, jnp.float32(-1e+30))
    row_max = lax.optimization_barrier(jnp.max(scores, axis=-1, keepdims=True))
    raised = jnp.exp(scores - row_max)
    weights_soft = (raised / lax.optimization_barrier(jnp.sum(raised, axis=-1, keepdims=True))).astype(jnp.bfloat16)
    attention_output = jnp.einsum('rhqk,rkd->rqhd', weights_soft.astype(jnp.float32), value_three)
    live_rows = (position[None, :] < input_lengths[:, None])[:, :, None, None]
    attention_output = jnp.where(live_rows, attention_output, jnp.float32(0.0))
    return attention_output.astype(jnp.bfloat16).reshape(rollouts_here * slot_len, num_heads * head_size)

def learner_block_step(normalized_rows, projected_rows, gradient_rows, input_lengths, adapter_down, adapter_up):
    query_total_width = adapter_up.shape[1]
    head_size = (projected_rows.shape[1] - query_total_width) // 2
    adapter_lowrank = jnp.dot(normalized_rows, adapter_down, preferred_element_type=jnp.float32).astype(jnp.bfloat16)
    query_rows = (projected_rows[:, :query_total_width] + ADAPTER_SCALE * jnp.dot(adapter_lowrank, adapter_up, preferred_element_type=jnp.float32)).astype(jnp.bfloat16)
    keys_rows = projected_rows[:, query_total_width:query_total_width + head_size].astype(jnp.bfloat16)
    values_rows = projected_rows[:, query_total_width + head_size:].astype(jnp.bfloat16)
    attention_output, pullback = jax.vjp(lambda query_in: attention(query_in, keys_rows, values_rows, input_lengths), query_rows)
    query_gradient = pullback(gradient_rows)[0]
    up_gradient = ADAPTER_SCALE * lax.dot_general(adapter_lowrank, query_gradient, (((0,), (0,)), ((), ())), preferred_element_type=jnp.float32)
    lowrank_gradient = (ADAPTER_SCALE * lax.dot_general(query_gradient, adapter_up, (((1,), (1,)), ((), ())), preferred_element_type=jnp.float32)).astype(jnp.bfloat16)
    down_gradient = lax.dot_general(normalized_rows, lowrank_gradient, (((0,), (0,)), ((), ())), preferred_element_type=jnp.float32)
    return (attention_output, down_gradient, up_gradient)

def reference(hidden_input, input_norm_gain, joined_weight, joined_bias, adapter_down, adapter_up, advantage, output_gradient, lengths, assignment):
    num_blocks = ROLLOUTS // ROLL_DEV
    query_total_width = QUERY_HEADS * HEAD_WIDTH

    def block_step(totals, inputs):
        block_x, block_grad, block_adv, block_length = inputs
        normalized_rows = normalize(block_x, input_norm_gain).reshape(ROLL_DEV * L, MODEL_WIDTH_DIM)
        projected_rows = jnp.dot(normalized_rows, joined_weight, preferred_element_type=jnp.float32) + joined_bias.astype(jnp.float32)
        gradient_rows = weigh_grad(block_grad, block_adv, block_length).reshape(ROLL_DEV * L, query_total_width)
        attention_output, down_gradient, up_gradient = learner_block_step(normalized_rows, projected_rows, gradient_rows, block_length, adapter_down, adapter_up)
        return ((totals[0] + down_gradient, totals[1] + up_gradient), attention_output.reshape(ROLL_DEV, L, query_total_width))
    start_sums = (jnp.zeros((MODEL_WIDTH_DIM, ADAPTER_RANK), jnp.float32), jnp.zeros((ADAPTER_RANK, query_total_width), jnp.float32))
    (down_gradient, up_gradient), attention_output = lax.scan(block_step, start_sums, (hidden_input.reshape(num_blocks, ROLL_DEV, L, MODEL_WIDTH_DIM), output_gradient.reshape(num_blocks, ROLL_DEV, L, query_total_width), advantage.reshape(num_blocks, ROLL_DEV), lengths.reshape(num_blocks, ROLL_DEV)))
    attention_output = attention_output.reshape(ROLLOUTS, L, query_total_width)
    rollout_index = jnp.arange(ROLLOUTS, dtype=jnp.int32)
    fsdp_column = rollout_index // ROLL_DEV % N_FSDP
    source = rollout_index // (ROLL_DEV * N_FSDP)
    earlier_same = (fsdp_column[:, None] == fsdp_column[None, :]) & (assignment[:, None] == assignment[None, :]) & (source[None, :] < source[:, None])
    slot_rank = lax.optimization_barrier(jnp.sum(earlier_same.astype(jnp.int32), axis=1)).astype(jnp.int32)
    target_row = ((assignment * N_FSDP + fsdp_column) * ROLL_DEV + slot_rank).astype(jnp.int32)
    att_out = jnp.zeros_like(attention_output).at[target_row].set(attention_output)
    return (att_out, down_gradient, up_gradient)
```

```python
import jax
import jax.numpy as jnp
from jax import lax
from jax.sharding import PartitionSpec as P

EPSILON = 1e-06
ADAPTER_SCALE = 2.0


def normalize(hidden_rows, gain):
    hidden_wide = hidden_rows.astype(jnp.float32)
    scale_rows = lax.rsqrt(jnp.mean(hidden_wide * hidden_wide, axis=-1, keepdims=True) + EPSILON)
    return (hidden_wide * scale_rows * gain).astype(jnp.bfloat16)


def weigh_grad(gradient_rows, adv_rows, length_rows):
    factor = adv_rows / length_rows.astype(jnp.float32)
    return (gradient_rows.astype(jnp.float32) * factor[:, None, None]).astype(jnp.bfloat16)


def attention(query_rows, keys_rows, values_rows, input_lengths):
    rollouts_here = input_lengths.shape[0]
    slot_len = query_rows.shape[0] // rollouts_here
    head_size = keys_rows.shape[1]
    num_heads = query_rows.shape[1] // head_size
    query_four = query_rows.reshape(rollouts_here, slot_len, num_heads, head_size).astype(
        jnp.float32
    )
    key_three = keys_rows.reshape(rollouts_here, slot_len, head_size).astype(jnp.float32)
    value_three = values_rows.reshape(rollouts_here, slot_len, head_size).astype(jnp.float32)
    scores = jnp.einsum("rqhd,rkd->rhqk", query_four, key_three) * head_size ** (-0.5)
    position = jnp.arange(slot_len, dtype=jnp.int32)
    visible = (position[None, None, None, :] <= position[None, None, :, None]) & (
        position[None, None, None, :] < input_lengths[:, None, None, None]
    )
    scores = jnp.where(visible, scores, jnp.float32(-1e30))
    row_max = jnp.max(scores, axis=-1, keepdims=True)
    raised = jnp.exp(scores - row_max)
    weights_soft = (raised / jnp.sum(raised, axis=-1, keepdims=True)).astype(jnp.bfloat16)
    attention_output = jnp.einsum("rhqk,rkd->rqhd", weights_soft.astype(jnp.float32), value_three)
    live_rows = (position[None, :] < input_lengths[:, None])[:, :, None, None]
    attention_output = jnp.where(live_rows, attention_output, jnp.float32(0.0))
    return attention_output.astype(jnp.bfloat16).reshape(
        rollouts_here * slot_len, num_heads * head_size
    )


def learner_block_step(
    normalized_rows, projected_rows, gradient_rows, input_lengths, adapter_down, adapter_up
):
    query_total_width = adapter_up.shape[1]
    head_size = (projected_rows.shape[1] - query_total_width) // 2
    adapter_lowrank = jnp.dot(
        normalized_rows, adapter_down, preferred_element_type=jnp.float32
    ).astype(jnp.bfloat16)
    query_rows = (
        projected_rows[:, :query_total_width]
        + ADAPTER_SCALE * jnp.dot(adapter_lowrank, adapter_up, preferred_element_type=jnp.float32)
    ).astype(jnp.bfloat16)
    keys_rows = projected_rows[:, query_total_width : query_total_width + head_size].astype(
        jnp.bfloat16
    )
    values_rows = projected_rows[:, query_total_width + head_size :].astype(jnp.bfloat16)
    attention_output, pullback = jax.vjp(
        lambda query_in: attention(query_in, keys_rows, values_rows, input_lengths), query_rows
    )
    query_gradient = pullback(gradient_rows)[0]
    up_gradient = ADAPTER_SCALE * lax.dot_general(
        adapter_lowrank,
        query_gradient,
        (((0,), (0,)), ((), ())),
        preferred_element_type=jnp.float32,
    )
    lowrank_gradient = (
        ADAPTER_SCALE
        * lax.dot_general(
            query_gradient, adapter_up, (((1,), (1,)), ((), ())), preferred_element_type=jnp.float32
        )
    ).astype(jnp.bfloat16)
    down_gradient = lax.dot_general(
        normalized_rows,
        lowrank_gradient,
        (((0,), (0,)), ((), ())),
        preferred_element_type=jnp.float32,
    )
    return (attention_output, down_gradient, up_gradient)


def on_device(
    hidden_input,
    input_norm_gain,
    joined_weight,
    joined_bias,
    adapter_down,
    adapter_up,
    advantage,
    output_gradient,
    lengths,
    assignment,
):
    rollouts_here, slot_len, model_width = hidden_input.shape
    dp_size = lax.axis_size("dp")
    query_total_width = adapter_up.shape[1]
    weighted_grad = weigh_grad(output_gradient, advantage, lengths)
    normalized_rows = normalize(hidden_input, input_norm_gain).reshape(-1, model_width)
    projected_rows = jnp.dot(
        normalized_rows,
        lax.all_gather(joined_weight, "fsdp", axis=0, tiled=True),
        preferred_element_type=jnp.float32,
    ) + joined_bias.astype(jnp.float32)
    attention_output, down_gradient, up_gradient = learner_block_step(
        normalized_rows,
        projected_rows,
        weighted_grad.reshape(normalized_rows.shape[0], query_total_width),
        lengths,
        adapter_down,
        adapter_up,
    )
    targets = assignment[None, :] == jnp.arange(dp_size, dtype=jnp.int32)[:, None]
    slots = jnp.dot(
        targets.astype(jnp.bfloat16),
        attention_output.reshape(rollouts_here, -1),
        preferred_element_type=jnp.float32,
    ).astype(jnp.bfloat16)
    arrived = lax.all_to_all(slots, "dp", split_axis=0, concat_axis=0, tiled=True)
    sent = jnp.sum(targets.astype(jnp.int32), axis=1)
    filled = lax.all_to_all(sent, "dp", split_axis=0, concat_axis=0, tiled=True) > 0
    slot_rank = jnp.cumsum(filled.astype(jnp.int32)) - 1
    select_table = (
        slot_rank[None, :] == jnp.arange(rollouts_here, dtype=jnp.int32)[:, None]
    ) & filled[None, :]
    att_out = (
        jnp.dot(select_table.astype(jnp.bfloat16), arrived, preferred_element_type=jnp.float32)
        .astype(jnp.bfloat16)
        .reshape(rollouts_here, slot_len, query_total_width)
    )
    column_a, column_b = lax.psum((down_gradient, up_gradient), "fsdp")
    share_a, share_b = (
        lax.psum_scatter(column_a, "dp", scatter_dimension=0, tiled=True),
        lax.psum_scatter(column_b, "dp", scatter_dimension=1, tiled=True),
    )
    return (att_out, share_a, share_b)


def solution(mesh):
    in_specs = (
        P(("dp", "fsdp"), None, None),
        P(),
        P("fsdp", None),
        P(),
        P(),
        P(),
        P(("dp", "fsdp")),
        P(("dp", "fsdp"), None, None),
        P(("dp", "fsdp")),
        P(("dp", "fsdp")),
    )
    out_specs = (P(("dp", "fsdp"), None, None), P("dp", None), P(None, "dp"))
    return jax.shard_map(
        on_device, mesh=mesh, in_specs=in_specs, out_specs=out_specs, check_vma=False
    )
```

```python
import functools

import jax
import jax.numpy as jnp
from jax import lax
from jax.experimental import pallas as pl
from jax.experimental.pallas import tpu as pltpu
from jax.sharding import PartitionSpec as P

EPSILON = 1e-06
ADAPTER_SCALE = 2.0
MESH = pl.DeviceIdType.MESH
NT = (((1,), (1,)), ((), ()))
TN = (((0,), (0,)), ((), ()))

SCHEDULE = (
    ((0, 1, 0, 2), (1, 3, 0, 6), (2, 0, 1, 0), (3, 0, 1, 4)),
    ((0, 1, 0, 0), (1, 3, 0, 2), (2, 0, 1, 6), (3, 0, 1, 2)),
    ((0, 1, 0, 4), (1, 3, 0, 4), (2, 0, 1, 3), (3, 1, 1, 2), (4, 0, 1, 1), (5, 3, 0, 7)),
    ((0, 1, 0, 6), (1, 3, 0, 0), (2, 1, 1, 0), (3, 0, 1, 5), (4, 0, 1, 7), (5, 1, 0, 3)),
    ((0, 1, 0, 7), (1, 3, 1, 0), (2, 1, 1, 4), (3, 3, 1, 2), (4, 3, 0, 5), (5, 1, 1, 3)),
    ((0, 2, 0, 6), (1, 2, 0, 0), (2, 3, 1, 4), (3, 1, 1, 6), (4, 1, 0, 1), (5, 1, 1, 1)),
    ((0, 1, 0, 5), (1, 2, 0, 2), (2, 3, 1, 7), (3, 3, 1, 6), (4, 3, 1, 1), (5, 1, 1, 5)),
    ((0, 2, 1, 4), (1, 2, 0, 4), (2, 2, 1, 6), (3, 3, 1, 5), (4, 3, 1, 3), (5, 2, 0, 1)),
    ((0, 2, 0, 5), (1, 3, 0, 3), (2, 1, 1, 7), (3, 3, 0, 1), (4, 2, 0, 7), (5, 2, 0, 3)),
    ((0, 2, 1, 3), (1, 2, 1, 2), (2, 2, 1, 1), (3, 2, 1, 0), (4, 2, 1, 7), (5, 2, 1, 5)),
)
ENTRIES = tuple((t,) + e for t, row in enumerate(SCHEDULE) for e in row)
N_ENTRIES = len(ENTRIES)
GAP = 2
PIECE = 64
GROUP = 256


def source_of(link, dx, dy, v):
    if link == 0:
        return (dx + 3) % 4, dy, v
    if link == 1:
        return (dx + 1) % 4, dy, v
    if link < 4:
        return dx, 1 - dy, v
    return dx, dy, v ^ 1


def group_plan():
    done = {}
    for t, _, dx, dy, v in ENTRIES:
        key = (dx, dy, v // 4)
        done[key] = max(done.get(key, 0), t)
    return done


GROUP_DONE = group_plan()


def lookup(index, values):
    out = jnp.int32(values[0])
    for i in range(1, len(values)):
        out = jnp.where(index == i, jnp.int32(values[i]), out)
    return out


def kernel(
    len_ref, assign_ref, adv_ref, hid_ref, gain_ref, w_ref, bias_ref, ad_ref, up_ref, og_ref,
    att_out, down_out, up_out,
    hbuf, nbuf, mnorm, wbuf, adbuf, ogbuf, acc, ssq, qbuf, kbuf, vbuf, low2, attb, pbuf, qg, lg,
    flags, pay_s, rec_s, pay_a, rec_a, pay_b, rec_b, pay_c, rec_c,
    hsem, lsem, wsend, wrecv, csend, crecv, msem, fsem, frecv, ssem, srecv, asem, arecv, bsem,
    brecv, gsem, grecv,
):
    me_d, me_f = lax.axis_index("dp"), lax.axis_index("fsdp")
    z, yh = me_d // 2, me_d % 2
    yl, x, c = me_f // 8, (me_f // 2) % 4, me_f % 2
    y = yh * 2 + yl
    par = z % 2
    chip = me_f // 2
    mate_f = me_f + 1 - 2 * c
    mate = (me_d, mate_f)

    def at(z_, y_, x_):
        return ((z_ % 8) * 2 + (y_ % 4) // 2, ((y_ % 4) % 2) * 8 + (x_ % 4) * 2 + c)

    receivers = (
        at(z, y, x + 3), at(z, y, x + 1), at(z, y + 3, x), at(z, y + 1, x), at(z + 7, y, x), at(z + 1, y, x),
    )
    cross = at(z, y + 1 - 2 * (1 - yl) + 4, x)
    f_peers = [(me_d, (me_f + k) % 16) for k in range(1, 16)]
    d_peers = [((me_d + k) % 16, me_f) for k in range(1, 16)]

    barrier = pltpu.get_barrier_semaphore()
    for peer in f_peers + d_peers + [cross]:
        pl.semaphore_signal(barrier, inc=1, device_id=peer, device_id_type=MESH)

    def hidden_copy(g):
        return pltpu.make_async_copy(
            hid_ref.at[:, pl.ds(pl.multiple_of(g * GROUP, GROUP), GROUP)], hbuf.at[g], hsem.at[g]
        )

    def start_hidden(g, carry):
        hidden_copy(g).start()
        return carry

    lax.fori_loop(0, 32, start_hidden, 0)
    local = [
        pltpu.make_async_copy(w_ref, wbuf.at[me_f], lsem.at[0]),
        pltpu.make_async_copy(ad_ref, adbuf, lsem.at[1]),
        pltpu.make_async_copy(og_ref, ogbuf, lsem.at[2]),
    ]
    for copy in local:
        copy.start()
    ssq[...] = jnp.zeros_like(ssq)
    for r in range(8):
        flags[me_d, pl.ds(r, 1), :] = jnp.full((1, 128), assign_ref[r], jnp.int32)

    pl.semaphore_wait(barrier, 31)

    def shard(dx, dy, core):
        yy = yl + dy - 2 * yl * dy
        return yy * 8 + ((x + dx) % 4) * 2 + core

    def rows_of(v):
        k = v + par if v % 2 == 0 else v - par
        return pl.ds(pl.multiple_of(k * PIECE, PIECE), PIECE)

    def piece_send(e):
        _, link, dx, dy, v = ENTRIES[e]
        sx, sy, sv = source_of(link, dx, dy, v)
        f, rows = shard(sx, sy, c), rows_of(sv)
        own = (sx, sy) == (0, 0)
        return pltpu.make_async_remote_copy(
            src_ref=w_ref.at[rows] if own else wbuf.at[f, rows],
            dst_ref=wbuf.at[f, rows],
            send_sem=wsend.at[e], recv_sem=wrecv.at[e],
            device_id=receivers[link], device_id_type=MESH,
        )

    def piece_landing(e):
        _, link, dx, dy, v = ENTRIES[e]
        spot = wbuf.at[shard(dx, dy, c), rows_of(v)]
        return pltpu.make_async_remote_copy(
            src_ref=spot, dst_ref=spot, send_sem=wsend.at[e], recv_sem=wrecv.at[e],
            device_id=mate, device_id_type=MESH,
        )

    def core_send(dx, dy, h):
        i = (dx * 2 + dy) * 2 + h
        f = shard(dx, dy, c)
        rows = pl.ds(h * GROUP, GROUP)
        own = (dx, dy) == (0, 0)
        return pltpu.make_async_remote_copy(
            src_ref=w_ref.at[rows] if own else wbuf.at[f, rows],
            dst_ref=wbuf.at[f, rows],
            send_sem=csend.at[i], recv_sem=crecv.at[i],
            device_id=mate, device_id_type=MESH,
        )

    def core_landing(dx, dy, h):
        i = (dx * 2 + dy) * 2 + h
        spot = wbuf.at[shard(dx, dy, 1 - c), pl.ds(h * GROUP, GROUP)]
        return pltpu.make_async_remote_copy(
            src_ref=spot, dst_ref=spot, send_sem=csend.at[i], recv_sem=crecv.at[i],
            device_id=mate, device_id_type=MESH,
        )

    def multiply(items):
        fx = [i[0] for i in items]
        fy = [i[1] for i in items]
        fh = [i[2] for i in items]
        fm = [i[3] for i in items]

        def body(i, carry):
            mine = lookup(i, fm)
            f = shard(lookup(i, fx), lookup(i, fy), c * mine + (1 - c) * (1 - mine))
            h = lookup(i, fh)
            rows = pl.ds(pl.multiple_of(h * GROUP, GROUP), GROUP)
            acc[...] += jnp.dot(nbuf[f * 2 + h], wbuf[f, rows, :], preferred_element_type=jnp.float32)
            return carry

        lax.fori_loop(0, len(items), body, 0)

    def sum_squares(g, carry):
        hidden_copy(g).wait()
        wide = hbuf[g].astype(jnp.float32)
        squared = wide * wide
        ssq[...] += squared[:, :128] + squared[:, 128:]
        return carry

    def scale_group(g, carry):
        gain = gain_ref[:, pl.ds(pl.multiple_of(g * GROUP, GROUP), GROUP)]
        nbuf[g] = (hbuf[g].astype(jnp.float32) * ssq[:, :1] * gain).astype(jnp.bfloat16)
        return carry

    def lora_group(g, carry):
        low2[...] += jnp.dot(nbuf[g], adbuf[g], preferred_element_type=jnp.float32)
        return carry

    flag_copies = [
        pltpu.make_async_remote_copy(
            src_ref=flags.at[me_d], dst_ref=flags.at[me_d], send_sem=fsem.at[k], recv_sem=frecv.at[k],
            device_id=d_peers[k], device_id_type=MESH,
        )
        for k in range(15)
    ]
    norm_copies = [
        pltpu.make_async_remote_copy(
            src_ref=nbuf.at[2 * d + 1 - c], dst_ref=mnorm.at[d], send_sem=msem.at[0, d], recv_sem=msem.at[1, d],
            device_id=mate, device_id_type=MESH,
        )
        for d in range(16)
    ]

    by_step = [[e for e in range(N_ENTRIES) if ENTRIES[e][0] == t] for t in range(len(SCHEDULE))]
    ready = [(0, 0, 0, 1), (0, 0, 1, 1)]
    mates = {0: [(0, 0, 0), (0, 0, 1)]}
    n_steps = len(SCHEDULE) + GAP
    bias_row = bias_ref[...].astype(jnp.float32)
    acc[...] = jnp.broadcast_to(bias_row, acc.shape)
    low2[...] = jnp.zeros_like(low2)
    for t in range(n_steps):
        if t >= GAP:
            for e in by_step[t - GAP]:
                piece_landing(e).wait_recv()
        if t < len(SCHEDULE):
            for e in by_step[t]:
                piece_send(e).start()
        if t == 0:
            core_send(0, 0, 0).start()
            core_send(0, 0, 1).start()
        for key, done in GROUP_DONE.items():
            if done == t - GAP:
                core_send(*key).start()
                ready.append(key + (1,))
                mates.setdefault(t, []).append(key)
        if t == 1:
            for copy in flag_copies:
                copy.start()
            lax.fori_loop(0, 32, sum_squares, 0)
            mean = jnp.sum(ssq[...], axis=1, keepdims=True) * (1.0 / 8192.0)
            ssq[...] = jnp.broadcast_to(lax.rsqrt(mean + EPSILON), ssq.shape)
        if t == 2:
            lax.fori_loop(0, 16, scale_group, 0)
        if t == 3:
            lax.fori_loop(16, 32, scale_group, 0)
            for copy in norm_copies:
                copy.start()
        if t == 4:
            local[1].wait()
            lax.fori_loop(0, 32, lora_group, 0)
            local[0].wait()
        if t >= 5:
            for s in [s for s in mates if s < t]:
                for key in mates.pop(s):
                    core_landing(*key).wait_recv()
                    ready.append(key + (0,))
            if ready:
                multiply(ready)
                ready = []
    last = [key for s in mates for key in mates[s]]
    for key in last:
        core_landing(*key).wait_recv()
    if last:
        multiply([key + (0,) for key in last])

    low = low2[...].astype(jnp.bfloat16)
    low_wide = jnp.concatenate([low, low], axis=1)
    lora = jnp.dot(low, up_ref[...], preferred_element_type=jnp.float32)
    qbuf[...] = (acc[:, :512] + ADAPTER_SCALE * lora).astype(jnp.bfloat16)
    kbuf[...] = acc[:, 512:640].astype(jnp.bfloat16)
    vbuf[...] = acc[:, 640:].astype(jnp.bfloat16)
    row = lax.broadcasted_iota(jnp.int32, (128, 128), 0)
    col = lax.broadcasted_iota(jnp.int32, (128, 128), 1)
    same = (row // 32) == (col // 32)
    causal = same & ((col % 32) <= (row % 32))
    scale = 128 ** (-0.5)

    def spread(ref, half, where, kind):
        out = jnp.full((128, 128), ref[half * 4].astype(kind), kind)
        for r in range(1, 4):
            out = jnp.where(where // 32 == r, jnp.full((128, 128), ref[half * 4 + r].astype(kind), kind), out)
        return out

    lives = []
    for half in range(2):
        rows = slice(half * 128, half * 128 + 128)
        visible = causal & ((col % 32) < spread(len_ref, half, col, jnp.int32))
        live = (row % 32) < spread(len_ref, half, row, jnp.int32)
        lives.append(live)
        for h in range(4):
            cols = slice(h * 128, h * 128 + 128)
            scores = lax.dot_general(qbuf[rows, cols], kbuf[rows, :], NT, preferred_element_type=jnp.float32)
            scores = jnp.where(visible, scores * scale, jnp.float32(-1e30))
            raised = jnp.exp(scores - jnp.max(scores, axis=-1, keepdims=True))
            soft = raised / jnp.sum(raised, axis=-1, keepdims=True)
            pbuf[half * 4 + h] = soft
            out = jnp.dot(soft.astype(jnp.bfloat16), vbuf[rows, :], preferred_element_type=jnp.float32)
            out = jnp.where(live, out, 0.0).astype(jnp.bfloat16)
            attb[half * 4 : half * 4 + 4, :, cols] = out.reshape(4, 32, 128)

    def fill_slot(d, carry):
        which = jnp.int32(0)
        for r in range(1, 8):
            which = jnp.where(assign_ref[r] == d, jnp.int32(r), which)
        pay_s[d] = attb[which]
        return carry

    lax.fori_loop(0, 16, fill_slot, 0)
    rec_s[me_d] = pay_s[me_d]
    slot_copies = [
        pltpu.make_async_remote_copy(
            src_ref=pay_s.at[d_peers[k][0]], dst_ref=rec_s.at[me_d], send_sem=ssem.at[k], recv_sem=srecv.at[k],
            device_id=d_peers[k], device_id_type=MESH,
        )
        for k in range(15)
    ]
    for copy in slot_copies:
        copy.start()

    local[2].wait()
    for half in range(2):
        rows = slice(half * 128, half * 128 + 128)
        factor = spread(adv_ref, half, row, jnp.float32) / spread(len_ref, half, row, jnp.float32)
        for h in range(4):
            cols = slice(h * 128, h * 128 + 128)
            weighted = (ogbuf[rows, cols].astype(jnp.float32) * factor).astype(jnp.bfloat16)
            weighted = jnp.where(lives[half], weighted.astype(jnp.float32), 0.0).astype(jnp.bfloat16)
            dsoft = lax.dot_general(weighted, vbuf[rows, :], NT, preferred_element_type=jnp.float32)
            dsoft = dsoft.astype(jnp.bfloat16).astype(jnp.float32)
            soft = pbuf[half * 4 + h]
            inner = jnp.sum(dsoft * soft, axis=-1, keepdims=True)
            dscores = (soft * (dsoft - inner) * scale).astype(jnp.bfloat16)
            dquery = jnp.dot(dscores, kbuf[rows, :], preferred_element_type=jnp.float32)
            qg[rows, cols] = dquery.astype(jnp.bfloat16)
    low_grad = ADAPTER_SCALE * lax.dot_general(up_ref[...], qg[...], NT, preferred_element_type=jnp.float32)
    lg[0] = low_grad.astype(jnp.bfloat16)
    lg_copy = pltpu.make_async_remote_copy(
        src_ref=lg.at[0], dst_ref=lg.at[1], send_sem=msem.at[0, 16], recv_sem=msem.at[1, 16],
        device_id=mate, device_id_type=MESH,
    )
    lg_copy.start()
    up_grad = ADAPTER_SCALE * lax.dot_general(qg[...], low_wide, TN, preferred_element_type=jnp.float32)
    up_four = up_grad.reshape(16, 2, 16, 128)
    lane = lax.broadcasted_iota(jnp.int32, (16, 16, 128), 2)
    pay_b[:, 1] = jnp.where(lane < 64, up_four[:, 0], up_four[:, 1]).astype(jnp.bfloat16)
    for copy in norm_copies:
        copy.wait()
    lg_copy.wait()

    def down_slice(d, carry):
        part = jnp.dot(lg[0], nbuf[2 * d + c], preferred_element_type=jnp.float32)
        part += jnp.dot(lg[1], mnorm[d], preferred_element_type=jnp.float32)
        part = part.astype(jnp.bfloat16)
        for i in range(4):
            for j in range(2):
                pay_a[j * 4 + i, d] = part[i * 16 : i * 16 + 16, j * 128 : j * 128 + 128]
        return carry

    lax.fori_loop(0, 16, down_slice, 0)
    a_copies = [
        pltpu.make_async_remote_copy(
            src_ref=pay_a.at[(chip + k) % 8], dst_ref=rec_a.at[k - 1], send_sem=asem.at[k - 1],
            recv_sem=arecv.at[k - 1], device_id=(me_d, ((chip + k) % 8) * 2 + c), device_id_type=MESH,
        )
        for k in range(1, 8)
    ]
    for copy in a_copies:
        copy.start()
    for e in range(N_ENTRIES):
        piece_send(e).wait_send()
    for key in [(0, 0, 0), (0, 0, 1)] + list(GROUP_DONE):
        core_send(*key).wait_send()
    for copy in flag_copies:
        copy.wait()
    for copy in a_copies:
        copy.wait()
    total = pay_a[chip].astype(jnp.float32)
    for k in range(7):
        total += rec_a[k].astype(jnp.float32)
    pay_b[:, 0] = total.astype(jnp.bfloat16)
    b_copies = [
        pltpu.make_async_remote_copy(
            src_ref=pay_b.at[d_peers[k][0]], dst_ref=rec_b.at[k], send_sem=bsem.at[k], recv_sem=brecv.at[k],
            device_id=d_peers[k], device_id_type=MESH,
        )
        for k in range(15)
    ]
    for copy in b_copies:
        copy.start()

    for copy in slot_copies:
        copy.wait()
    held = [jnp.sum((flags[s] == me_d).astype(jnp.float32), axis=0, keepdims=True) for s in range(16)]
    before = [jnp.zeros((1, 128), jnp.float32)]
    for s in range(15):
        before.append(before[-1] + held[s])
    for i in range(8):
        picked = jnp.zeros((32, 512), jnp.bfloat16)
        for s in range(i, i + 9):
            take = jnp.where(before[s] == float(i), held[s], 0.0).astype(jnp.bfloat16)
            picked += rec_s[s] * jnp.concatenate([take] * 4, axis=1)
        att_out[i] = picked

    for copy in b_copies:
        copy.wait()
    total = pay_b[me_d].astype(jnp.float32)
    for k in range(15):
        total += rec_b[k].astype(jnp.float32)
    pay_c[...] = total
    rec_c[me_f] = total
    c_copies = [
        pltpu.make_async_remote_copy(
            src_ref=pay_c, dst_ref=rec_c.at[me_f], send_sem=gsem.at[k], recv_sem=grecv.at[k],
            device_id=f_peers[k], device_id_type=MESH,
        )
        for k in range(15)
    ]
    for copy in c_copies:
        copy.start()
    for copy in c_copies:
        copy.wait()
    for f in range(16):
        j, i, core = f // 8, (f // 2) % 4, f % 2
        down_out[i * 16 : i * 16 + 16, core * 256 + j * 128 : core * 256 + j * 128 + 128] = rec_c[f, 0]
    total = rec_c[0, 1]
    for f in range(1, 16):
        total += rec_c[f, 1]
    up_out[...] = total


def on_device(
    hidden_input, input_norm_gain, joined_weight, joined_bias, adapter_down, adapter_up, advantage,
    output_gradient, lengths, assignment,
):
    bf16, f32 = jnp.bfloat16, jnp.float32
    dma = pltpu.SemaphoreType.DMA
    smem = pl.BlockSpec(memory_space=pltpu.SMEM)
    vmem = pl.BlockSpec(memory_space=pltpu.VMEM)
    hbm = pl.BlockSpec(memory_space=pl.ANY)
    att, down, up = pl.pallas_call(
        kernel,
        out_shape=(
            jax.ShapeDtypeStruct((8, 32, 512), bf16),
            jax.ShapeDtypeStruct((64, 512), f32),
            jax.ShapeDtypeStruct((16, 128), f32),
        ),
        in_specs=[smem, smem, smem, hbm, vmem, hbm, vmem, hbm, vmem, hbm],
        out_specs=(vmem, vmem, vmem),
        scratch_shapes=[
            pltpu.VMEM((32, 256, 256), bf16),
            pltpu.VMEM((32, 256, 256), bf16),
            pltpu.VMEM((16, 256, 256), bf16),
            pltpu.VMEM((16, 512, 768), bf16),
            pltpu.VMEM((32, 256, 64), bf16),
            pltpu.VMEM((256, 512), bf16),
            pltpu.VMEM((256, 768), f32),
            pltpu.VMEM((256, 128), f32),
            pltpu.VMEM((256, 512), bf16),
            pltpu.VMEM((256, 128), bf16),
            pltpu.VMEM((256, 128), bf16),
            pltpu.VMEM((256, 64), f32),
            pltpu.VMEM((8, 32, 512), bf16),
            pltpu.VMEM((8, 128, 128), f32),
            pltpu.VMEM((256, 512), bf16),
            pltpu.VMEM((2, 64, 256), bf16),
            pltpu.VMEM((16, 8, 128), jnp.int32),
            pltpu.VMEM((16, 32, 512), bf16),
            pltpu.VMEM((16, 32, 512), bf16),
            pltpu.VMEM((8, 16, 16, 128), bf16),
            pltpu.VMEM((7, 16, 16, 128), bf16),
            pltpu.VMEM((16, 2, 16, 128), bf16),
            pltpu.VMEM((15, 2, 16, 128), bf16),
            pltpu.VMEM((2, 16, 128), f32),
            pltpu.VMEM((16, 2, 16, 128), f32),
            dma((32,)), dma((3,)), dma((N_ENTRIES,)), dma((N_ENTRIES,)), dma((16,)), dma((16,)),
            dma((2, 17)), dma((15,)), dma((15,)), dma((15,)), dma((15,)), dma((7,)), dma((7,)),
            dma((15,)), dma((15,)), dma((15,)), dma((15,)),
        ],
        compiler_params=pltpu.CompilerParams(
            collective_id=0, has_side_effects=True, vmem_limit_bytes=56 * 2**20
        ),
        name="block",
    )(
        lengths,
        assignment,
        advantage,
        hidden_input.reshape(256, 8192),
        input_norm_gain.reshape(1, 8192),
        joined_weight,
        joined_bias.reshape(1, 768),
        adapter_down.reshape(32, 256, 64),
        adapter_up,
        output_gradient.reshape(256, 512),
    )
    return att, down.T, up.reshape(16, 2, 64).transpose(2, 1, 0).reshape(64, 32)


def solution(mesh):
    in_specs = (
        P(("dp", "fsdp"), None, None),
        P(),
        P("fsdp", None),
        P(),
        P(),
        P(),
        P(("dp", "fsdp")),
        P(("dp", "fsdp"), None, None),
        P(("dp", "fsdp")),
        P(("dp", "fsdp")),
    )
    out_specs = (P(("dp", "fsdp"), None, None), P("dp", None), P(None, "dp"))
    return jax.shard_map(
        on_device, mesh=mesh, in_specs=in_specs, out_specs=out_specs, check_vma=False
    )
```

```python
import jax
import jax.numpy as jnp
from jax import lax
from jax.experimental import pallas as pl
from jax.experimental.pallas import tpu as pltpu
from jax.sharding import PartitionSpec as P

EPSILON = 1e-06
ADAPTER_SCALE = 2.0
MESH = pl.DeviceIdType.MESH
NT = (((1,), (1,)), ((), ()))
TN = (((0,), (0,)), ((), ()))

SCHEDULE = (
    ((0, 1, 0, 2), (1, 3, 0, 6), (2, 0, 1, 0), (3, 0, 1, 4)),
    ((0, 1, 0, 0), (1, 3, 0, 2), (2, 0, 1, 6), (3, 0, 1, 2)),
    ((0, 1, 0, 4), (1, 3, 0, 4), (2, 0, 1, 3), (3, 1, 1, 2), (4, 0, 1, 1), (5, 3, 0, 7)),
    ((0, 1, 0, 6), (1, 3, 0, 0), (2, 1, 1, 0), (3, 0, 1, 5), (4, 0, 1, 7), (5, 1, 0, 3)),
    ((0, 1, 0, 7), (1, 3, 1, 0), (2, 1, 1, 4), (3, 3, 1, 2), (4, 3, 0, 5), (5, 1, 1, 3)),
    ((0, 2, 0, 6), (1, 2, 0, 0), (2, 3, 1, 4), (3, 1, 1, 6), (4, 1, 0, 1), (5, 1, 1, 1)),
    ((0, 1, 0, 5), (1, 2, 0, 2), (2, 3, 1, 7), (3, 3, 1, 6), (4, 3, 1, 1), (5, 1, 1, 5)),
    ((0, 2, 1, 4), (1, 2, 0, 4), (2, 2, 1, 6), (3, 3, 1, 5), (4, 3, 1, 3), (5, 2, 0, 1)),
    ((0, 2, 0, 5), (1, 3, 0, 3), (2, 1, 1, 7), (3, 3, 0, 1), (4, 2, 0, 7), (5, 2, 0, 3)),
    ((0, 2, 1, 3), (1, 2, 1, 2), (2, 2, 1, 1), (3, 2, 1, 0), (4, 2, 1, 7), (5, 2, 1, 5)),
)
ENTRIES = tuple((t,) + e for t, row in enumerate(SCHEDULE) for e in row)
N_ENTRIES = len(ENTRIES)
GAP = 2
PIECE = 64
ORDER = (7, 8, 9, 10, 6, 5, 11, 12, 4, 3, 13, 14, 2, 1, 15, 0)
CHUNK = 4
GROUP = 256


def source_of(link, dx, dy, v):
    if link == 0:
        return (dx + 3) % 4, dy, v
    if link == 1:
        return (dx + 1) % 4, dy, v
    if link < 4:
        return dx, 1 - dy, v
    return dx, dy, v ^ 1


def group_plan():
    done = {}
    for t, _, dx, dy, v in ENTRIES:
        key = (dx, dy, v // 4)
        done[key] = max(done.get(key, 0), t)
    return done


GROUP_DONE = group_plan()


def lookup(index, values):
    out = jnp.int32(values[0])
    for i in range(1, len(values)):
        out = jnp.where(index == i, jnp.int32(values[i]), out)
    return out


def kernel(
    len_hbm, assign_hbm, adv_hbm, hid_ref, gain_hbm, w_ref, bias_hbm, ad_hbm, up_hbm, og_hbm,
    att_out, rec_c,
    len_ref, assign_ref, adv_ref, gain_ref, bias_ref, ad_ref, up_ref, og_ref,
    hbuf, nbuf, mnorm, wbuf, acc, ssq, qbuf, kbuf, vbuf, low2, attb, pbuf, qg, lg,
    flags, pay_s, rec_s, ordered, pay_a, rec_a, pay_b, rec_b, pay_c,
    tokens, hsem, lsem, wsend, wrecv, csend, crecv, msem, fsem, frecv, ssem, srecv, asem, arecv, bsem,
    brecv, gsem, grecv,
):
    me_d, me_f = lax.axis_index("dp"), lax.axis_index("fsdp")
    z, yh = me_d // 2, me_d % 2
    yl, x, c = me_f // 8, (me_f // 2) % 4, me_f % 2
    y = yh * 2 + yl
    par = z % 2
    chip = me_f // 2
    mate_f = me_f + 1 - 2 * c
    mate = (me_d, mate_f)

    def at(z_, y_, x_):
        return ((z_ % 8) * 2 + (y_ % 4) // 2, ((y_ % 4) % 2) * 8 + (x_ % 4) * 2 + c)

    receivers = (
        at(z, y, x + 3), at(z, y, x + 1), at(z, y + 3, x), at(z, y + 1, x), at(z + 7, y, x), at(z + 1, y, x),
    )
    neighbours = receivers + (mate,)
    f_peers = [(me_d, (me_f + k) % 16) for k in range(1, 16)]
    d_peers = [((me_d + k) % 16, me_f) for k in range(1, 16)]

    barrier = pltpu.get_barrier_semaphore()
    for peer in neighbours:
        pl.semaphore_signal(barrier, inc=1, device_id=peer, device_id_type=MESH)

    def hidden_copy(g):
        return pltpu.make_async_copy(
            hid_ref.at[:, pl.ds(pl.multiple_of(g * GROUP, GROUP), GROUP)], hbuf.at[g], hsem.at[g]
        )

    def start_hidden(g, carry):
        hidden_copy(g).start()
        return carry

    lax.fori_loop(0, 32, start_hidden, 0)
    local = [
        pltpu.make_async_copy(src, dst, lsem.at[i])
        for i, (src, dst) in enumerate((
            (w_ref, wbuf.at[me_f]), (ad_hbm, ad_ref), (og_hbm, og_ref), (len_hbm, len_ref), (assign_hbm, assign_ref),
            (adv_hbm, adv_ref), (gain_hbm, gain_ref), (bias_hbm, bias_ref), (up_hbm, up_ref),
        ))
    ]
    for copy in local:
        copy.start()
    ssq[...] = jnp.zeros_like(ssq)
    low2[...] = jnp.zeros_like(low2)

    pl.semaphore_wait(barrier, 7)

    def send_tokens(i):
        for peer in neighbours:
            pl.semaphore_signal(tokens.at[i], inc=1, device_id=peer, device_id_type=MESH)

    def take_tokens(i):
        pl.semaphore_wait(tokens.at[i], 7)

    def shard(dx, dy, core):
        yy = yl + dy - 2 * yl * dy
        return yy * 8 + ((x + dx) % 4) * 2 + core

    def rows_of(v):
        k = v + par if v % 2 == 0 else v - par
        return pl.ds(pl.multiple_of(k * PIECE, PIECE), PIECE)

    def piece_send(e):
        _, link, dx, dy, v = ENTRIES[e]
        sx, sy, sv = source_of(link, dx, dy, v)
        f, rows = shard(sx, sy, c), rows_of(sv)
        own = (sx, sy) == (0, 0)
        return pltpu.make_async_remote_copy(
            src_ref=w_ref.at[rows] if own else wbuf.at[f, rows],
            dst_ref=wbuf.at[f, rows],
            send_sem=wsend.at[e], recv_sem=wrecv.at[e],
            device_id=receivers[link], device_id_type=MESH,
        )

    def piece_landing(e):
        _, link, dx, dy, v = ENTRIES[e]
        spot = wbuf.at[shard(dx, dy, c), rows_of(v)]
        return pltpu.make_async_remote_copy(
            src_ref=spot, dst_ref=spot, send_sem=wsend.at[e], recv_sem=wrecv.at[e],
            device_id=mate, device_id_type=MESH,
        )

    def core_send(dx, dy, h):
        i = (dx * 2 + dy) * 2 + h
        f = shard(dx, dy, c)
        rows = pl.ds(h * GROUP, GROUP)
        own = (dx, dy) == (0, 0)
        return pltpu.make_async_remote_copy(
            src_ref=w_ref.at[rows] if own else wbuf.at[f, rows],
            dst_ref=wbuf.at[f, rows],
            send_sem=csend.at[i], recv_sem=crecv.at[i],
            device_id=mate, device_id_type=MESH,
        )

    def core_landing(dx, dy, h):
        i = (dx * 2 + dy) * 2 + h
        spot = wbuf.at[shard(dx, dy, 1 - c), pl.ds(h * GROUP, GROUP)]
        return pltpu.make_async_remote_copy(
            src_ref=spot, dst_ref=spot, send_sem=csend.at[i], recv_sem=crecv.at[i],
            device_id=mate, device_id_type=MESH,
        )

    def multiply(items):
        fx = [i[0] for i in items]
        fy = [i[1] for i in items]
        fh = [i[2] for i in items]
        fm = [i[3] for i in items]

        def body(i, carry):
            mine = lookup(i, fm)
            f = shard(lookup(i, fx), lookup(i, fy), c * mine + (1 - c) * (1 - mine))
            h = lookup(i, fh)
            rows = pl.ds(pl.multiple_of(h * GROUP, GROUP), GROUP)
            acc[...] += jnp.dot(nbuf[f * 2 + h], wbuf[f, rows, :], preferred_element_type=jnp.float32)
            return carry

        lax.fori_loop(0, len(items), body, 0)

    def sum_squares(g, carry):
        hidden_copy(g).wait()
        wide = hbuf[g].astype(jnp.float32)
        squared = wide * wide
        ssq[...] += squared[:, :128] + squared[:, 128:]
        return carry

    def scale_group(g, carry):
        gain = gain_ref[:, pl.ds(pl.multiple_of(g * GROUP, GROUP), GROUP)]
        nbuf[g] = (hbuf[g].astype(jnp.float32) * ssq[:, :1] * gain).astype(jnp.bfloat16)
        return carry

    def lora_group(g, carry):
        cols = pl.ds(pl.multiple_of(g * GROUP, GROUP), GROUP)
        low2[...] += lax.dot_general(nbuf[g], ad_ref[:, cols], NT, preferred_element_type=jnp.float32)
        return carry

    flag_copies = [
        pltpu.make_async_remote_copy(
            src_ref=flags.at[me_d], dst_ref=flags.at[me_d], send_sem=fsem.at[k], recv_sem=frecv.at[k],
            device_id=d_peers[k], device_id_type=MESH,
        )
        for k in range(15)
    ]
    norm_copies = [
        pltpu.make_async_remote_copy(
            src_ref=nbuf.at[2 * d + 1 - c], dst_ref=mnorm.at[d], send_sem=msem.at[0, d], recv_sem=msem.at[1, d],
            device_id=mate, device_id_type=MESH,
        )
        for d in range(16)
    ]

    by_step = [[e for e in range(N_ENTRIES) if ENTRIES[e][0] == t] for t in range(len(SCHEDULE))]
    ready = [(0, 0, 0, 1), (0, 0, 1, 1)]
    mates = {0: [(0, 0, 0), (0, 0, 1)]}
    n_steps = len(SCHEDULE) + GAP
    for t in range(n_steps):
        if t >= GAP:
            for e in by_step[t - GAP]:
                piece_landing(e).wait_recv()
        if t < len(SCHEDULE):
            for e in by_step[t]:
                piece_send(e).start()
        if 1 <= t <= 5:
            take_tokens(t - 1)
        if t < 5:
            send_tokens(t)
        if t == 0:
            core_send(0, 0, 0).start()
            core_send(0, 0, 1).start()
        for key, done in GROUP_DONE.items():
            if done == t - GAP:
                core_send(*key).start()
                ready.append(key + (1,))
                mates.setdefault(t, []).append(key)
        if t == 1:
            lax.fori_loop(0, 32, sum_squares, 0)
            mean = jnp.sum(ssq[...], axis=1, keepdims=True) * (1.0 / 8192.0)
            ssq[...] = jnp.broadcast_to(lax.rsqrt(mean + EPSILON), ssq.shape)
        if t == 2:
            local[6].wait()
            lax.fori_loop(0, 16, scale_group, 0)
        if t == 3:
            lax.fori_loop(16, 32, scale_group, 0)
            for copy in norm_copies:
                copy.start()
        if t == 4:
            local[1].wait()
            lax.fori_loop(0, 32, lora_group, 0)
            local[0].wait()
            local[7].wait()
            acc[...] = jnp.broadcast_to(bias_ref[...].astype(jnp.float32).reshape(1, 768), acc.shape)
        if t == 6:
            for i in (3, 4, 5, 8):
                local[i].wait()
            for r in range(8):
                flags[me_d, pl.ds(r, 1), :] = jnp.full((1, 128), assign_ref[r], jnp.int32)
            for copy in flag_copies:
                copy.start()
        if t >= 5:
            for s in [s for s in mates if s < t]:
                for key in mates.pop(s):
                    core_landing(*key).wait_recv()
                    ready.append(key + (0,))
            if ready:
                multiply(ready)
                ready = []
    last = [key for s in mates for key in mates[s]]
    for key in last:
        core_landing(*key).wait_recv()
    if last:
        multiply([key + (0,) for key in last])

    low = low2[...].astype(jnp.bfloat16)
    low_wide = jnp.concatenate([low, low], axis=1)
    lora = jnp.dot(low, up_ref[...], preferred_element_type=jnp.float32)
    qbuf[...] = (acc[:, :512] + ADAPTER_SCALE * lora).astype(jnp.bfloat16)
    kbuf[...] = acc[:, 512:640].astype(jnp.bfloat16)
    vbuf[...] = acc[:, 640:].astype(jnp.bfloat16)
    row = lax.broadcasted_iota(jnp.int32, (128, 128), 0)
    col = lax.broadcasted_iota(jnp.int32, (128, 128), 1)
    same = (row // 32) == (col // 32)
    causal = same & ((col % 32) <= (row % 32))
    scale = 128 ** (-0.5)

    def spread(ref, half, where, kind):
        out = jnp.full((128, 128), ref[half * 4].astype(kind), kind)
        for r in range(1, 4):
            out = jnp.where(where // 32 == r, jnp.full((128, 128), ref[half * 4 + r].astype(kind), kind), out)
        return out

    lives = []
    for half in range(2):
        rows = slice(half * 128, half * 128 + 128)
        visible = causal & ((col % 32) < spread(len_ref, half, col, jnp.int32))
        live = (row % 32) < spread(len_ref, half, row, jnp.int32)
        lives.append(live)
        for h in range(4):
            cols = slice(h * 128, h * 128 + 128)
            scores = lax.dot_general(qbuf[rows, cols], kbuf[rows, :], NT, preferred_element_type=jnp.float32)
            scores = jnp.where(visible, scores * scale, jnp.float32(-1e30))
            raised = jnp.exp(scores - jnp.max(scores, axis=-1, keepdims=True))
            soft = raised / jnp.sum(raised, axis=-1, keepdims=True)
            pbuf[half * 4 + h] = soft
            out = jnp.dot(soft.astype(jnp.bfloat16), vbuf[rows, :], preferred_element_type=jnp.float32)
            out = jnp.where(live, out, 0.0).astype(jnp.bfloat16)
            attb[half * 4 : half * 4 + 4, :, cols] = out.reshape(4, 32, 128)

    def fill_slot(d, carry):
        which = jnp.int32(0)
        for r in range(1, 8):
            which = jnp.where(assign_ref[r] == d, jnp.int32(r), which)
        pay_s[d] = attb[which]
        return carry

    lax.fori_loop(0, 16, fill_slot, 0)
    rec_s[me_d] = pay_s[me_d]
    slot_copies = [
        pltpu.make_async_remote_copy(
            src_ref=pay_s.at[d_peers[k][0]], dst_ref=rec_s.at[me_d], send_sem=ssem.at[k], recv_sem=srecv.at[k],
            device_id=d_peers[k], device_id_type=MESH,
        )
        for k in range(15)
    ]
    for copy in slot_copies:
        copy.start()

    local[2].wait()
    for half in range(2):
        rows = slice(half * 128, half * 128 + 128)
        factor = spread(adv_ref, half, row, jnp.float32) / spread(len_ref, half, row, jnp.float32)
        for h in range(4):
            cols = slice(h * 128, h * 128 + 128)
            weighted = (og_ref[rows, cols].astype(jnp.float32) * factor).astype(jnp.bfloat16)
            weighted = jnp.where(lives[half], weighted.astype(jnp.float32), 0.0).astype(jnp.bfloat16)
            dsoft = lax.dot_general(weighted, vbuf[rows, :], NT, preferred_element_type=jnp.float32)
            dsoft = dsoft.astype(jnp.bfloat16).astype(jnp.float32)
            soft = pbuf[half * 4 + h]
            inner = jnp.sum(dsoft * soft, axis=-1, keepdims=True)
            dscores = (soft * (dsoft - inner) * scale).astype(jnp.bfloat16)
            dquery = jnp.dot(dscores, kbuf[rows, :], preferred_element_type=jnp.float32)
            qg[rows, cols] = dquery.astype(jnp.bfloat16)
    low_grad = ADAPTER_SCALE * lax.dot_general(up_ref[...], qg[...], NT, preferred_element_type=jnp.float32)
    lg[0] = low_grad.astype(jnp.bfloat16)
    lg_copy = pltpu.make_async_remote_copy(
        src_ref=lg.at[0], dst_ref=lg.at[1], send_sem=msem.at[0, 16], recv_sem=msem.at[1, 16],
        device_id=mate, device_id_type=MESH,
    )
    lg_copy.start()
    up_grad = ADAPTER_SCALE * lax.dot_general(qg[...], low_wide, TN, preferred_element_type=jnp.float32)
    up_four = up_grad.reshape(16, 2, 16, 128)
    lane = lax.broadcasted_iota(jnp.int32, (16, 16, 128), 2)
    ordered[...] = jnp.where(lane < 64, up_four[:, 0], up_four[:, 1]).astype(jnp.bfloat16)
    for copy in norm_copies:
        copy.wait()
    lg_copy.wait()

    def down_slice(i, carry):
        d = (me_d + lookup(i, ORDER)) % 16
        part = jnp.dot(lg[0], nbuf[2 * d + c], preferred_element_type=jnp.float32)
        part += jnp.dot(lg[1], mnorm[d], preferred_element_type=jnp.float32)
        part = part.astype(jnp.bfloat16)
        for i2 in range(4):
            for j2 in range(2):
                pay_a[j2 * 4 + i2, i] = part[i2 * 16 : i2 * 16 + 16, j2 * 128 : j2 * 128 + 128]
        return carry

    def a_copy(q, k):
        span = pl.ds(q * CHUNK, CHUNK)
        return pltpu.make_async_remote_copy(
            src_ref=pay_a.at[(chip + k) % 8, span], dst_ref=rec_a.at[k - 1, span], send_sem=asem.at[q, k - 1],
            recv_sem=arecv.at[q, k - 1], device_id=(me_d, ((chip + k) % 8) * 2 + c), device_id_type=MESH,
        )

    chunks = range(16 // CHUNK)
    for q in chunks:
        lax.fori_loop(q * CHUNK, (q + 1) * CHUNK, down_slice, 0)
        for k in range(1, 8):
            a_copy(q, k).start()
    for e in range(N_ENTRIES):
        piece_send(e).wait_send()
    for key in [(0, 0, 0), (0, 0, 1)] + list(GROUP_DONE):
        core_send(*key).wait_send()
    for copy in flag_copies:
        copy.wait()
    b_copies = [
        pltpu.make_async_remote_copy(
            src_ref=pay_b.at[i], dst_ref=rec_b.at[i], send_sem=bsem.at[i], recv_sem=brecv.at[i],
            device_id=((me_d + ORDER[i]) % 16, me_f), device_id_type=MESH,
        )
        for i in range(15)
    ]
    for q in chunks:
        span = pl.ds(q * CHUNK, CHUNK)
        for k in range(1, 8):
            a_copy(q, k).wait()
        total = pay_a[chip, span].astype(jnp.float32)
        for k in range(7):
            total += rec_a[k, span].astype(jnp.float32)
        pay_b[span, 0] = total.astype(jnp.bfloat16)
        for i in range(q * CHUNK, (q + 1) * CHUNK):
            pay_b[i, 1] = ordered[(me_d + ORDER[i]) % 16]
            if i < 15:
                b_copies[i].start()

    for copy in slot_copies:
        copy.wait()
    held = [jnp.sum((flags[s] == me_d).astype(jnp.float32), axis=0, keepdims=True) for s in range(16)]
    before = [jnp.zeros((1, 128), jnp.float32)]
    for s in range(15):
        before.append(before[-1] + held[s])
    for i in range(8):
        picked = jnp.zeros((32, 512), jnp.bfloat16)
        for s in range(i, i + 9):
            take = jnp.where(before[s] == float(i), held[s], 0.0).astype(jnp.bfloat16)
            picked += rec_s[s] * jnp.concatenate([take] * 4, axis=1)
        attb[i] = picked
    att_copy = pltpu.make_async_copy(attb, att_out, lsem.at[9])
    att_copy.start()

    for copy in b_copies:
        copy.wait()
    total = pay_b[15].astype(jnp.float32)
    for k in range(15):
        total += rec_b[k].astype(jnp.float32)
    pay_c[...] = total.astype(jnp.bfloat16)
    c_copies = [
        pltpu.make_async_remote_copy(
            src_ref=pay_c, dst_ref=rec_c.at[me_f], send_sem=gsem.at[k], recv_sem=grecv.at[k],
            device_id=f_peers[k], device_id_type=MESH,
        )
        for k in range(15)
    ]
    for copy in c_copies:
        copy.start()
    own_copy = pltpu.make_async_copy(pay_c, rec_c.at[me_f], lsem.at[10])
    own_copy.start()
    for copy in c_copies:
        copy.wait()
    own_copy.wait()
    att_copy.wait()


def assemble(att_ref, sums_ref, att_out, down_out, up_out):
    att_out[...] = att_ref[...]
    for f in range(16):
        j, i, core = f // 8, (f // 2) % 4, f % 2
        down_out[i * 16 : i * 16 + 16, core * 256 + j * 128 : core * 256 + j * 128 + 128] = sums_ref[f, 0].astype(
            jnp.float32
        )
    total = sums_ref[0, 1].astype(jnp.float32)
    for f in range(1, 16):
        total += sums_ref[f, 1].astype(jnp.float32)
    up_out[:16, :] = total[:, :64]
    up_out[16:, :] = total[:, 64:]


def on_device(
    hidden_input, input_norm_gain, joined_weight, joined_bias, adapter_down, adapter_up, advantage,
    output_gradient, lengths, assignment,
):
    bf16, f32 = jnp.bfloat16, jnp.float32
    dma = pltpu.SemaphoreType.DMA
    vmem = pl.BlockSpec(memory_space=pltpu.VMEM)
    hbm = pl.BlockSpec(memory_space=pl.ANY)
    att, sums = pl.pallas_call(
        kernel,
        out_shape=(jax.ShapeDtypeStruct((8, 32, 512), bf16), jax.ShapeDtypeStruct((16, 2, 16, 128), bf16)),
        in_specs=[hbm] * 10,
        out_specs=(hbm, hbm),
        scratch_shapes=[
            pltpu.SMEM((8,), jnp.int32),
            pltpu.SMEM((8,), jnp.int32),
            pltpu.SMEM((8,), f32),
            pltpu.VMEM((1, 8192), f32),
            pltpu.VMEM((768,), bf16),
            pltpu.VMEM((64, 8192), bf16),
            pltpu.VMEM((64, 512), bf16),
            pltpu.VMEM((256, 512), bf16),
            pltpu.VMEM((32, 256, 256), bf16),
            pltpu.VMEM((32, 256, 256), bf16),
            pltpu.VMEM((16, 256, 256), bf16),
            pltpu.VMEM((16, 512, 768), bf16),
            pltpu.VMEM((256, 768), f32),
            pltpu.VMEM((256, 128), f32),
            pltpu.VMEM((256, 512), bf16),
            pltpu.VMEM((256, 128), bf16),
            pltpu.VMEM((256, 128), bf16),
            pltpu.VMEM((256, 64), f32),
            pltpu.VMEM((8, 32, 512), bf16),
            pltpu.VMEM((8, 128, 128), f32),
            pltpu.VMEM((256, 512), bf16),
            pltpu.VMEM((2, 64, 256), bf16),
            pltpu.VMEM((16, 8, 128), jnp.int32),
            pltpu.VMEM((16, 32, 512), bf16),
            pltpu.VMEM((16, 32, 512), bf16),
            pltpu.VMEM((16, 16, 128), bf16),
            pltpu.VMEM((8, 16, 16, 128), bf16),
            pltpu.VMEM((7, 16, 16, 128), bf16),
            pltpu.VMEM((16, 2, 16, 128), bf16),
            pltpu.VMEM((15, 2, 16, 128), bf16),
            pltpu.VMEM((2, 16, 128), bf16),
            pltpu.SemaphoreType.REGULAR((5,)),
            dma((32,)), dma((11,)), dma((N_ENTRIES,)), dma((N_ENTRIES,)), dma((16,)), dma((16,)),
            dma((2, 17)), dma((15,)), dma((15,)), dma((15,)), dma((15,)), dma((16 // CHUNK, 7)), dma((16 // CHUNK, 7)),
            dma((15,)), dma((15,)), dma((15,)), dma((15,)),
        ],
        compiler_params=pltpu.CompilerParams(
            collective_id=0, has_side_effects=True, vmem_limit_bytes=56 * 2**20
        ),
        name="block",
    )(
        lengths,
        assignment,
        advantage,
        hidden_input.reshape(256, 8192),
        input_norm_gain.reshape(1, 8192),
        joined_weight,
        joined_bias,
        adapter_down.T,
        adapter_up,
        output_gradient.reshape(256, 512),
    )
    att, down, up = pl.pallas_call(
        assemble,
        out_shape=(
            jax.ShapeDtypeStruct((8, 32, 512), bf16),
            jax.ShapeDtypeStruct((64, 512), f32),
            jax.ShapeDtypeStruct((32, 64), f32),
        ),
        in_specs=[vmem, vmem],
        out_specs=(vmem, vmem, vmem),
        name="assemble",
    )(att, sums)
    return att, down.T, up.T


def solution(mesh):
    in_specs = (
        P(("dp", "fsdp"), None, None),
        P(),
        P("fsdp", None),
        P(),
        P(),
        P(),
        P(("dp", "fsdp")),
        P(("dp", "fsdp"), None, None),
        P(("dp", "fsdp")),
        P(("dp", "fsdp")),
    )
    out_specs = (P(("dp", "fsdp"), None, None), P("dp", None), P(None, "dp"))
    return jax.shard_map(
        on_device, mesh=mesh, in_specs=in_specs, out_specs=out_specs, check_vma=False
    )
```

```python
import jax
import jax.numpy as jnp
from jax import lax
from jax.experimental import pallas as pl
from jax.experimental.pallas import tpu as pltpu
from jax.sharding import PartitionSpec as P

EPSILON = 1e-06
ADAPTER_SCALE = 2.0
MESH = pl.DeviceIdType.MESH
NT = (((1,), (1,)), ((), ()))
TN = (((0,), (0,)), ((), ()))

SCHEDULE = (
    ((0, 1, 0, 4), (1, 3, 0, 0), (2, 0, 1, 4), (3, 0, 1, 6)),
    ((0, 1, 0, 0), (1, 3, 0, 4), (2, 0, 1, 0), (3, 0, 1, 2)),
    ((0, 1, 0, 2), (1, 3, 0, 6), (2, 0, 1, 5), (3, 0, 1, 1)),
    ((0, 1, 1, 6), (1, 3, 0, 2), (2, 1, 1, 4), (3, 3, 1, 0), (4, 1, 0, 5), (5, 3, 0, 1)),
    ((0, 1, 0, 6), (1, 3, 1, 2), (2, 1, 1, 0), (3, 0, 1, 7), (4, 1, 0, 1), (5, 3, 0, 5)),
    ((0, 2, 0, 4), (1, 2, 0, 0), (2, 1, 1, 2), (3, 3, 1, 6), (4, 3, 0, 7), (5, 1, 0, 3)),
    ((0, 2, 1, 4), (1, 2, 0, 2), (2, 0, 1, 3), (3, 3, 1, 4), (4, 3, 1, 1), (5, 1, 1, 7)),
    ((0, 1, 0, 7), (1, 2, 0, 6), (2, 1, 1, 5), (3, 1, 1, 1), (4, 3, 0, 3), (5, 3, 1, 3)),
    ((0, 2, 1, 6), (1, 2, 1, 2), (2, 3, 1, 7), (3, 2, 1, 0), (4, 2, 0, 5), (5, 2, 0, 1)),
    ((0, 2, 1, 7), (1, 2, 0, 7), (2, 1, 1, 3), (3, 3, 1, 5), (4, 2, 0, 3), (5, 2, 1, 5)),
    ((0, 2, 1, 1), (1, 2, 1, 3)),
)
ENTRIES = tuple((t,) + e for t, row in enumerate(SCHEDULE) for e in row)
N_ENTRIES = len(ENTRIES)
GAP = 3
PIECE = 64
ORDER = (7, 8, 9, 10, 6, 5, 11, 12, 4, 3, 13, 14, 2, 1, 15, 0)
CHUNK = 4
GROUP = 256


def source_of(link, dx, dy, v):
    if link == 0:
        return (dx + 3) % 4, dy, v
    if link == 1:
        return (dx + 1) % 4, dy, v
    if link < 4:
        return dx, 1 - dy, v
    return dx, dy, v ^ 1


def group_plan():
    done = {}
    for t, _, dx, dy, v in ENTRIES:
        key = (dx, dy, v // 4)
        done[key] = max(done.get(key, 0), t)
    return done


GROUP_DONE = group_plan()
AHEAD = 1


def issue_plan():
    slot_of = {(dx, dy, v): t for t, _, dx, dy, v in ENTRIES}
    plan = [[] for _ in range(len(SCHEDULE) + GAP)]
    latest = {}
    for e, (t, link, dx, dy, v) in enumerate(ENTRIES):
        sx, sy, sv = source_of(link, dx, dy, v)
        have = 0 if (sx, sy) == (0, 0) else slot_of[sx, sy, sv] + GAP
        latest[link] = max(have, t - AHEAD, latest.get(link, 0))
        plan[latest[link]].append(e)
    return plan


ISSUE = issue_plan()


def lookup(index, values):
    out = jnp.int32(values[0])
    for i in range(1, len(values)):
        out = jnp.where(index == i, jnp.int32(values[i]), out)
    return out


def kernel(
    len_hbm, assign_hbm, adv_hbm, hid_ref, gain_hbm, w_ref, bias_hbm, ad_hbm, up_hbm, og_hbm,
    att_out, rec_c,
    len_ref, assign_ref, adv_ref, gain_ref, bias_ref, ad_ref, up_ref, og_ref,
    hbuf, nbuf, wbuf, acc, part_acc, ssq, kbuf, vbuf, low2, attb, pbuf, qg, lg,
    flags, pay_s, rec_s, ordered, pay_a, rec_a, pay_b, rec_b, pay_c,
    tokens, hsem, lsem, wsend, wrecv, msem, fsem, frecv, ssem, srecv, asem, arecv, bsem,
    brecv, gsem, grecv,
):
    me_d, me_f = lax.axis_index("dp"), lax.axis_index("fsdp")
    z, yh = me_d // 2, me_d % 2
    yl, x, c = me_f // 8, (me_f // 2) % 4, me_f % 2
    y = yh * 2 + yl
    par = z % 2
    chip = me_f // 2
    mate_f = me_f + 1 - 2 * c
    mate = (me_d, mate_f)

    def at(z_, y_, x_):
        return ((z_ % 8) * 2 + (y_ % 4) // 2, ((y_ % 4) % 2) * 8 + (x_ % 4) * 2 + c)

    receivers = (
        at(z, y, x + 3), at(z, y, x + 1), at(z, y + 3, x), at(z, y + 1, x), at(z + 7, y, x), at(z + 1, y, x),
    )
    neighbours = receivers + (mate,)
    f_peers = [(me_d, (me_f + k) % 16) for k in range(1, 16)]
    d_peers = [((me_d + k) % 16, me_f) for k in range(1, 16)]

    barrier = pltpu.get_barrier_semaphore()
    for peer in neighbours:
        pl.semaphore_signal(barrier, inc=1, device_id=peer, device_id_type=MESH)

    def hidden_copy(g):
        return pltpu.make_async_copy(
            hid_ref.at[:, pl.ds(pl.multiple_of(g * GROUP, GROUP), GROUP)], hbuf.at[g], hsem.at[g]
        )

    def start_hidden(g, carry):
        hidden_copy(g).start()
        return carry

    lax.fori_loop(0, 32, start_hidden, 0)
    local = [
        pltpu.make_async_copy(src, dst, lsem.at[i])
        for i, (src, dst) in enumerate((
            (w_ref, wbuf.at[chip]), (ad_hbm, ad_ref), (og_hbm, og_ref), (len_hbm, len_ref), (assign_hbm, assign_ref),
            (adv_hbm, adv_ref), (gain_hbm, gain_ref), (bias_hbm, bias_ref), (up_hbm, up_ref),
        ))
    ]
    for copy in local:
        copy.start()
    ssq[...] = jnp.zeros_like(ssq)
    low2[...] = jnp.zeros_like(low2)

    pl.semaphore_wait(barrier, 7)

    def send_tokens(i):
        for peer in neighbours:
            pl.semaphore_signal(tokens.at[i], inc=1, device_id=peer, device_id_type=MESH)

    def take_tokens(i):
        pl.semaphore_wait(tokens.at[i], 7)

    def shard(dx, dy):
        return (yl + dy - 2 * yl * dy) * 4 + (x + dx) % 4

    def rows_of(v):
        k = v + par if v % 2 == 0 else v - par
        return pl.ds(pl.multiple_of(k * PIECE, PIECE), PIECE)

    def piece_send(e):
        _, link, dx, dy, v = ENTRIES[e]
        sx, sy, sv = source_of(link, dx, dy, v)
        f, rows = shard(sx, sy), rows_of(sv)
        own = (sx, sy) == (0, 0)
        return pltpu.make_async_remote_copy(
            src_ref=w_ref.at[rows] if own else wbuf.at[f, rows],
            dst_ref=wbuf.at[f, rows],
            send_sem=wsend.at[e], recv_sem=wrecv.at[e],
            device_id=receivers[link], device_id_type=MESH,
        )

    def piece_landing(e):
        _, link, dx, dy, v = ENTRIES[e]
        spot = wbuf.at[shard(dx, dy), rows_of(v)]
        return pltpu.make_async_remote_copy(
            src_ref=spot, dst_ref=spot, send_sem=wsend.at[e], recv_sem=wrecv.at[e],
            device_id=mate, device_id_type=MESH,
        )

    def multiply(items, rows):
        def body(i, carry):
            j = shard(lookup(i, [item[0] for item in items]), lookup(i, [item[1] for item in items]))
            h = lookup(i, [item[2] for item in items])
            span = pl.ds(pl.multiple_of(h * GROUP, GROUP), GROUP)
            acc[rows, :] += jnp.dot(
                nbuf[(2 * j + c) * 2 + h, rows, :], wbuf[j, span, :], preferred_element_type=jnp.float32
            )
            return carry

        lax.fori_loop(0, len(items), body, 0)

    def sum_squares(g, carry):
        hidden_copy(g).wait()
        wide = hbuf[g].astype(jnp.float32)
        squared = wide * wide
        ssq[...] += squared[:, :128] + squared[:, 128:]
        return carry

    def scale_group(g, carry):
        gain = gain_ref[:, pl.ds(pl.multiple_of(g * GROUP, GROUP), GROUP)]
        nbuf[g, :256, :] = (hbuf[g].astype(jnp.float32) * ssq[:, :1] * gain).astype(jnp.bfloat16)
        return carry

    def lora_group(g, carry):
        cols = pl.ds(pl.multiple_of(g * GROUP, GROUP), GROUP)
        low2[...] += lax.dot_general(nbuf[g, :256, :], ad_ref[:, cols], NT, preferred_element_type=jnp.float32)
        return carry

    flag_copies = [
        pltpu.make_async_remote_copy(
            src_ref=flags.at[me_d], dst_ref=flags.at[me_d], send_sem=fsem.at[k], recv_sem=frecv.at[k],
            device_id=d_peers[k], device_id_type=MESH,
        )
        for k in range(15)
    ]
    def norm_copy(i):
        if i < 8:
            place = pl.ds((2 * i + 1 - c) * 2, 2)
        else:
            place = pl.ds((2 * (i - 8) + c) * 2 + 1 - c, 1)
        return pltpu.make_async_remote_copy(
            src_ref=nbuf.at[place, pl.ds(0, 256)], dst_ref=nbuf.at[place, pl.ds(256, 256)],
            send_sem=msem.at[0, i], recv_sem=msem.at[1, i], device_id=mate, device_id_type=MESH,
        )

    def part_copy(half):
        rows = pl.ds(half * 128, 128)
        return pltpu.make_async_remote_copy(
            src_ref=acc.at[pl.ds(256 + half * 128, 128)], dst_ref=part_acc.at[rows],
            send_sem=msem.at[0, 17 + half], recv_sem=msem.at[1, 17 + half], device_id=mate, device_id_type=MESH,
        )

    by_step = [[e for e in range(N_ENTRIES) if ENTRIES[e][0] == t] for t in range(len(SCHEDULE))]
    ready = [(0, 0, 0), (0, 0, 1)]
    mine, others = slice(0, 256), slice(256, 512)
    n_steps = len(SCHEDULE) + GAP
    for t in range(n_steps):
        if t >= GAP:
            for e in by_step[t - GAP]:
                piece_landing(e).wait_recv()
        for e in ISSUE[t]:
            piece_send(e).start()
        if 1 <= t <= 5:
            take_tokens(t - 1)
        if t < 5:
            send_tokens(t)
        for key, done in GROUP_DONE.items():
            if done == t - GAP:
                ready.append(key)
        if t == 0:
            lax.fori_loop(0, 16, sum_squares, 0)
        if t == 1:
            lax.fori_loop(16, 32, sum_squares, 0)
            mean = jnp.sum(ssq[...], axis=1, keepdims=True) * (1.0 / 8192.0)
            ssq[...] = jnp.broadcast_to(lax.rsqrt(mean + EPSILON), ssq.shape)
            local[6].wait()
        if t == 2:
            lax.fori_loop(0, 16, scale_group, 0)
            for i in (0, 1, 2, 3, 8, 9, 10, 11):
                norm_copy(i).start()
        if t == 3:
            lax.fori_loop(16, 32, scale_group, 0)
            for i in (4, 5, 6, 7, 12, 13, 14, 15):
                norm_copy(i).start()
            local[1].wait()
        if t == 4:
            lax.fori_loop(0, 16, lora_group, 0)
        if t == 5:
            lax.fori_loop(16, 32, lora_group, 0)
            local[0].wait()
            local[7].wait()
            acc[mine, :] = jnp.broadcast_to(bias_ref[...].astype(jnp.float32).reshape(1, 768), (256, 768))
            acc[others, :] = jnp.zeros((256, 768), jnp.float32)
            for i in range(16):
                norm_copy(i).wait_recv()
        if t == 6:
            for i in (3, 4, 5, 8):
                local[i].wait()
            for r in range(8):
                flags[me_d, pl.ds(r, 1), :] = jnp.full((1, 128), assign_ref[r], jnp.int32)
            for copy in flag_copies:
                copy.start()
        if 6 <= t < n_steps - 1 and ready:
            multiply(ready, slice(0, 512))
            ready = []
    multiply(ready, others)
    part_copy(0).start()
    part_copy(1).start()
    multiply(ready, mine)

    low = low2[...].astype(jnp.bfloat16)
    low_wide = jnp.concatenate([low, low], axis=1)
    lora = jnp.dot(low, up_ref[...], preferred_element_type=jnp.float32)
    row = lax.broadcasted_iota(jnp.int32, (128, 128), 0)
    col = lax.broadcasted_iota(jnp.int32, (128, 128), 1)
    same = (row // 32) == (col // 32)
    causal = same & ((col % 32) <= (row % 32))
    scale = 128 ** (-0.5)
    heads = [slice(h * 128, h * 128 + 128) for h in range(4)]

    def spread(ref, half, where, kind):
        out = jnp.full((128, 128), ref[half * 4].astype(kind), kind)
        for r in range(1, 4):
            out = jnp.where(where // 32 == r, jnp.full((128, 128), ref[half * 4 + r].astype(kind), kind), out)
        return out

    lives = [(row % 32) < spread(len_ref, half, row, jnp.int32) for half in range(2)]
    seen = [causal & ((col % 32) < spread(len_ref, half, col, jnp.int32)) for half in range(2)]
    for half in range(2):
        rows = slice(half * 128, half * 128 + 128)
        part_copy(half).wait_recv()
        projected = acc[rows, :] + part_acc[rows, :]
        queries = (projected[:, :512] + ADAPTER_SCALE * lora[rows, :]).astype(jnp.bfloat16)
        keys = projected[:, 512:640].astype(jnp.bfloat16)
        values = projected[:, 640:].astype(jnp.bfloat16)
        kbuf[rows, :] = keys
        vbuf[rows, :] = values
        scores = [lax.dot_general(queries[:, h], keys, NT, preferred_element_type=jnp.float32) for h in heads]
        scores = [jnp.where(seen[half], s * scale, jnp.float32(-1e30)) for s in scores]
        raised = [jnp.exp(s - jnp.max(s, axis=-1, keepdims=True)) for s in scores]
        soft = [r / jnp.sum(r, axis=-1, keepdims=True) for r in raised]
        outs = [jnp.dot(p.astype(jnp.bfloat16), values, preferred_element_type=jnp.float32) for p in soft]
        for i, h in enumerate(heads):
            pbuf[half * 4 + i] = soft[i]
            out = jnp.where(lives[half], outs[i], 0.0).astype(jnp.bfloat16)
            attb[half * 4 : half * 4 + 4, :, h] = out.reshape(4, 32, 128)

    def fill_slot(d, carry):
        which = jnp.int32(0)
        for r in range(1, 8):
            which = jnp.where(assign_ref[r] == d, jnp.int32(r), which)
        pay_s[d] = attb[which]
        return carry

    lax.fori_loop(0, 16, fill_slot, 0)
    rec_s[me_d] = pay_s[me_d]
    slot_copies = [
        pltpu.make_async_remote_copy(
            src_ref=pay_s.at[d_peers[k][0]], dst_ref=rec_s.at[me_d], send_sem=ssem.at[k], recv_sem=srecv.at[k],
            device_id=d_peers[k], device_id_type=MESH,
        )
        for k in range(15)
    ]
    for copy in slot_copies:
        copy.start()

    local[2].wait()
    for half in range(2):
        rows = slice(half * 128, half * 128 + 128)
        factor = spread(adv_ref, half, row, jnp.float32) / spread(len_ref, half, row, jnp.float32)
        keys, values = kbuf[rows, :], vbuf[rows, :]
        weighted = [(og_ref[rows, h].astype(jnp.float32) * factor).astype(jnp.bfloat16) for h in heads]
        weighted = [jnp.where(lives[half], w.astype(jnp.float32), 0.0).astype(jnp.bfloat16) for w in weighted]
        dsoft = [lax.dot_general(w, values, NT, preferred_element_type=jnp.float32) for w in weighted]
        dsoft = [d.astype(jnp.bfloat16).astype(jnp.float32) for d in dsoft]
        soft = [pbuf[half * 4 + i] for i in range(4)]
        inner = [jnp.sum(d * p, axis=-1, keepdims=True) for d, p in zip(dsoft, soft)]
        dscores = [(p * (d - i) * scale).astype(jnp.bfloat16) for d, p, i in zip(dsoft, soft, inner)]
        dquery = [jnp.dot(d, keys, preferred_element_type=jnp.float32) for d in dscores]
        for d, h in zip(dquery, heads):
            qg[rows, h] = d.astype(jnp.bfloat16)
    low_grad = ADAPTER_SCALE * lax.dot_general(up_ref[...], qg[...], NT, preferred_element_type=jnp.float32)
    lg[:, :256] = low_grad.astype(jnp.bfloat16)
    lg_copy = pltpu.make_async_remote_copy(
        src_ref=lg.at[:, pl.ds(0, 256)], dst_ref=lg.at[:, pl.ds(256, 256)], send_sem=msem.at[0, 16], recv_sem=msem.at[1, 16],
        device_id=mate, device_id_type=MESH,
    )
    lg_copy.start()
    up_grad = ADAPTER_SCALE * lax.dot_general(qg[...], low_wide, TN, preferred_element_type=jnp.float32)
    up_four = up_grad.reshape(16, 2, 16, 128)
    lane = lax.broadcasted_iota(jnp.int32, (16, 16, 128), 2)
    ordered[...] = jnp.where(lane < 64, up_four[:, 0], up_four[:, 1]).astype(jnp.bfloat16)
    lg_copy.wait()

    def down_slice(i, carry):
        d = (me_d + lookup(i, ORDER)) % 16
        part = jnp.dot(lg[...], nbuf[2 * d + c], preferred_element_type=jnp.float32).astype(jnp.bfloat16)
        for i2 in range(4):
            for j2 in range(2):
                pay_a[j2 * 4 + i2, i] = part[i2 * 16 : i2 * 16 + 16, j2 * 128 : j2 * 128 + 128]
        return carry

    def a_copy(q, k):
        span = pl.ds(q * CHUNK, CHUNK)
        return pltpu.make_async_remote_copy(
            src_ref=pay_a.at[(chip + k) % 8, span], dst_ref=rec_a.at[k - 1, span], send_sem=asem.at[q, k - 1],
            recv_sem=arecv.at[q, k - 1], device_id=(me_d, ((chip + k) % 8) * 2 + c), device_id_type=MESH,
        )

    chunks = range(16 // CHUNK)
    for q in chunks:
        lax.fori_loop(q * CHUNK, (q + 1) * CHUNK, down_slice, 0)
        for k in range(1, 8):
            a_copy(q, k).start()
    for e in range(N_ENTRIES):
        piece_send(e).wait_send()
    for i in range(16):
        norm_copy(i).wait_send()
    for half in range(2):
        part_copy(half).wait_send()
    for copy in flag_copies:
        copy.wait()
    b_copies = [
        pltpu.make_async_remote_copy(
            src_ref=pay_b.at[i], dst_ref=rec_b.at[i], send_sem=bsem.at[i], recv_sem=brecv.at[i],
            device_id=((me_d + ORDER[i]) % 16, me_f), device_id_type=MESH,
        )
        for i in range(15)
    ]
    for q in chunks:
        span = pl.ds(q * CHUNK, CHUNK)
        for k in range(1, 8):
            a_copy(q, k).wait()
        total = pay_a[chip, span].astype(jnp.float32)
        for k in range(7):
            total += rec_a[k, span].astype(jnp.float32)
        pay_b[span, 0] = total.astype(jnp.bfloat16)
        for i in range(q * CHUNK, (q + 1) * CHUNK):
            pay_b[i, 1] = ordered[(me_d + ORDER[i]) % 16]
            if i < 15:
                b_copies[i].start()

    for copy in slot_copies:
        copy.wait()
    held = [jnp.sum((flags[s] == me_d).astype(jnp.float32), axis=0, keepdims=True) for s in range(16)]
    before = [jnp.zeros((1, 128), jnp.float32)]
    for s in range(15):
        before.append(before[-1] + held[s])
    for i in range(8):
        picked = jnp.zeros((32, 512), jnp.bfloat16)
        for s in range(i, i + 9):
            take = jnp.where(before[s] == float(i), held[s], 0.0).astype(jnp.bfloat16)
            picked += rec_s[s] * jnp.concatenate([take] * 4, axis=1)
        attb[i] = picked
    att_copy = pltpu.make_async_copy(attb, att_out, lsem.at[9])
    att_copy.start()

    for copy in b_copies:
        copy.wait()
    total = pay_b[15].astype(jnp.float32)
    for k in range(15):
        total += rec_b[k].astype(jnp.float32)
    pay_c[...] = total.astype(jnp.bfloat16)
    c_copies = [
        pltpu.make_async_remote_copy(
            src_ref=pay_c, dst_ref=rec_c.at[me_f], send_sem=gsem.at[k], recv_sem=grecv.at[k],
            device_id=f_peers[k], device_id_type=MESH,
        )
        for k in range(15)
    ]
    for copy in c_copies:
        copy.start()
    own_copy = pltpu.make_async_copy(pay_c, rec_c.at[me_f], lsem.at[10])
    own_copy.start()
    for copy in c_copies:
        copy.wait()
    own_copy.wait()
    att_copy.wait()


def assemble(att_ref, sums_ref, att_out, down_out, up_out):
    att_out[...] = att_ref[...]
    for f in range(16):
        j, i, core = f // 8, (f // 2) % 4, f % 2
        down_out[i * 16 : i * 16 + 16, core * 256 + j * 128 : core * 256 + j * 128 + 128] = sums_ref[f, 0].astype(
            jnp.float32
        )
    total = sums_ref[0, 1].astype(jnp.float32)
    for f in range(1, 16):
        total += sums_ref[f, 1].astype(jnp.float32)
    up_out[:16, :] = total[:, :64]
    up_out[16:, :] = total[:, 64:]


def on_device(
    hidden_input, input_norm_gain, joined_weight, joined_bias, adapter_down, adapter_up, advantage,
    output_gradient, lengths, assignment,
):
    bf16, f32 = jnp.bfloat16, jnp.float32
    dma = pltpu.SemaphoreType.DMA
    vmem = pl.BlockSpec(memory_space=pltpu.VMEM)
    hbm = pl.BlockSpec(memory_space=pl.ANY)
    att, sums = pl.pallas_call(
        kernel,
        out_shape=(jax.ShapeDtypeStruct((8, 32, 512), bf16), jax.ShapeDtypeStruct((16, 2, 16, 128), bf16)),
        in_specs=[hbm] * 10,
        out_specs=(hbm, hbm),
        scratch_shapes=[
            pltpu.SMEM((8,), jnp.int32),
            pltpu.SMEM((8,), jnp.int32),
            pltpu.SMEM((8,), f32),
            pltpu.VMEM((1, 8192), f32),
            pltpu.VMEM((768,), bf16),
            pltpu.VMEM((64, 8192), bf16),
            pltpu.VMEM((64, 512), bf16),
            pltpu.VMEM((256, 512), bf16),
            pltpu.VMEM((32, 256, 256), bf16),
            pltpu.VMEM((32, 512, 256), bf16),
            pltpu.VMEM((8, 512, 768), bf16),
            pltpu.VMEM((512, 768), f32),
            pltpu.VMEM((256, 768), f32),
            pltpu.VMEM((256, 128), f32),
            pltpu.VMEM((256, 128), bf16),
            pltpu.VMEM((256, 128), bf16),
            pltpu.VMEM((256, 64), f32),
            pltpu.VMEM((8, 32, 512), bf16),
            pltpu.VMEM((8, 128, 128), f32),
            pltpu.VMEM((256, 512), bf16),
            pltpu.VMEM((64, 512), bf16),
            pltpu.VMEM((16, 8, 128), jnp.int32),
            pltpu.VMEM((16, 32, 512), bf16),
            pltpu.VMEM((16, 32, 512), bf16),
            pltpu.VMEM((16, 16, 128), bf16),
            pltpu.VMEM((8, 16, 16, 128), bf16),
            pltpu.VMEM((7, 16, 16, 128), bf16),
            pltpu.VMEM((16, 2, 16, 128), bf16),
            pltpu.VMEM((15, 2, 16, 128), bf16),
            pltpu.VMEM((2, 16, 128), bf16),
            pltpu.SemaphoreType.REGULAR((5,)),
            dma((32,)), dma((11,)), dma((N_ENTRIES,)), dma((N_ENTRIES,)),
            dma((2, 19)), dma((15,)), dma((15,)), dma((15,)), dma((15,)), dma((16 // CHUNK, 7)), dma((16 // CHUNK, 7)),
            dma((15,)), dma((15,)), dma((15,)), dma((15,)),
        ],
        compiler_params=pltpu.CompilerParams(
            collective_id=0, has_side_effects=True, vmem_limit_bytes=56 * 2**20
        ),
        name="block",
    )(
        lengths,
        assignment,
        advantage,
        hidden_input.reshape(256, 8192),
        input_norm_gain.reshape(1, 8192),
        joined_weight,
        joined_bias,
        adapter_down.T,
        adapter_up,
        output_gradient.reshape(256, 512),
    )
    att, down, up = pl.pallas_call(
        assemble,
        out_shape=(
            jax.ShapeDtypeStruct((8, 32, 512), bf16),
            jax.ShapeDtypeStruct((64, 512), f32),
            jax.ShapeDtypeStruct((32, 64), f32),
        ),
        in_specs=[vmem, vmem],
        out_specs=(vmem, vmem, vmem),
        name="assemble",
    )(att, sums)
    return att, down.T, up.T


def solution(mesh):
    in_specs = (
        P(("dp", "fsdp"), None, None),
        P(),
        P("fsdp", None),
        P(),
        P(),
        P(),
        P(("dp", "fsdp")),
        P(("dp", "fsdp"), None, None),
        P(("dp", "fsdp")),
        P(("dp", "fsdp")),
    )
    out_specs = (P(("dp", "fsdp"), None, None), P("dp", None), P(None, "dp"))
    return jax.shard_map(
        on_device, mesh=mesh, in_specs=in_specs, out_specs=out_specs, check_vma=False
    )
```

```python
import jax
import jax.numpy as jnp
from jax import lax
from jax.experimental import pallas as pl
from jax.experimental.pallas import tpu as pltpu
from jax.sharding import PartitionSpec as P

EPSILON = 1e-06
ADAPTER_SCALE = 2.0
MESH = pl.DeviceIdType.MESH
NT = (((1,), (1,)), ((), ()))
TN = (((0,), (0,)), ((), ()))

SCHEDULE = (
    ((0, 1, 0, 4), (1, 3, 0, 0), (2, 0, 1, 4), (3, 0, 1, 6)),
    ((0, 1, 0, 0), (1, 3, 0, 4), (2, 0, 1, 0), (3, 0, 1, 2)),
    ((0, 1, 0, 2), (1, 3, 0, 6), (2, 0, 1, 5), (3, 0, 1, 1)),
    ((0, 1, 1, 6), (1, 3, 0, 2), (2, 1, 1, 4), (3, 3, 1, 0), (4, 1, 0, 5), (5, 3, 0, 1)),
    ((0, 1, 0, 6), (1, 3, 1, 2), (2, 1, 1, 0), (3, 0, 1, 7), (4, 1, 0, 1), (5, 3, 0, 5)),
    ((0, 2, 0, 4), (1, 2, 0, 0), (2, 1, 1, 2), (3, 3, 1, 6), (4, 3, 0, 7), (5, 1, 0, 3)),
    ((0, 2, 1, 4), (1, 2, 0, 2), (2, 0, 1, 3), (3, 3, 1, 4), (4, 3, 1, 1), (5, 1, 1, 7)),
    ((0, 1, 0, 7), (1, 2, 0, 6), (2, 1, 1, 5), (3, 1, 1, 1), (4, 3, 0, 3), (5, 3, 1, 3)),
    ((0, 2, 1, 6), (1, 2, 1, 2), (2, 3, 1, 7), (3, 2, 1, 0), (4, 2, 0, 5), (5, 2, 0, 1)),
    ((0, 2, 1, 7), (1, 2, 0, 7), (2, 1, 1, 3), (3, 3, 1, 5), (4, 2, 0, 3), (5, 2, 1, 5)),
    ((0, 2, 1, 1), (1, 2, 1, 3)),
)
ENTRIES = tuple((t,) + e for t, row in enumerate(SCHEDULE) for e in row)
N_ENTRIES = len(ENTRIES)
GAP = 3
PIECE = 64
ORDER = (7, 8, 9, 10, 6, 5, 11, 12, 4, 3, 13, 14, 2, 1, 15)
Z_ORDER = (4, 3, 5, 2, 6, 1, 7, 0)
CHUNK = 4
GROUP = 256


def source_of(link, dx, dy, v):
    if link == 0:
        return (dx + 3) % 4, dy, v
    if link == 1:
        return (dx + 1) % 4, dy, v
    if link < 4:
        return dx, 1 - dy, v
    return dx, dy, v ^ 1


def group_plan():
    done = {}
    for t, _, dx, dy, v in ENTRIES:
        key = (dx, dy, v // 4)
        done[key] = max(done.get(key, 0), t)
    return done


GROUP_DONE = group_plan()
AHEAD = 1
LATE_FROM = len(SCHEDULE) - 1
LATE = tuple(key for key in GROUP_DONE if GROUP_DONE[key] >= LATE_FROM)
SPLIT = 6


def issue_plan():
    slot_of = {(dx, dy, v): t for t, _, dx, dy, v in ENTRIES}
    plan = [[] for _ in range(len(SCHEDULE) + GAP)]
    latest = {}
    for e, (t, link, dx, dy, v) in enumerate(ENTRIES):
        sx, sy, sv = source_of(link, dx, dy, v)
        have = 0 if (sx, sy) == (0, 0) else slot_of[sx, sy, sv] + GAP
        latest[link] = max(have, t - AHEAD, latest.get(link, 0))
        plan[latest[link]].append(e)
    return plan


ISSUE = issue_plan()


def lookup(index, values):
    out = jnp.int32(values[0])
    for i in range(1, len(values)):
        out = jnp.where(index == i, jnp.int32(values[i]), out)
    return out


def kernel(
    len_hbm, assign_hbm, adv_hbm, hid_ref, gain_hbm, w_ref, bias_hbm, ad_hbm, up_hbm, og_hbm,
    att_out, rec_c,
    len_ref, assign_ref, adv_ref, gain_ref, bias_ref, ad_ref, up_ref, og_ref,
    hbuf, nbuf, wbuf, wlate, acc, part_acc, ssq, kbuf, vbuf, low2, attb, pbuf, qg, lg,
    flags, pay_s, rec_s, ordered, pay_a, rec_a, pay_b, rec_b, pay_c,
    tokens, hsem, lsem, wsend, wrecv, psend, precv, msem, fsem, frecv, ssem, srecv, asem, arecv, bsem,
    brecv, gsem, grecv,
):
    me_d, me_f = lax.axis_index("dp"), lax.axis_index("fsdp")
    z, yh = me_d // 2, me_d % 2
    yl, x, c = me_f // 8, (me_f // 2) % 4, me_f % 2
    y = yh * 2 + yl
    par = z % 2
    chip = me_f // 2
    mate_f = me_f + 1 - 2 * c
    mate = (me_d, mate_f)

    def at(z_, y_, x_):
        return ((z_ % 8) * 2 + (y_ % 4) // 2, ((y_ % 4) % 2) * 8 + (x_ % 4) * 2 + c)

    receivers = (
        at(z, y, x + 3), at(z, y, x + 1), at(z, y + 3, x), at(z, y + 1, x), at(z + 7, y, x), at(z + 1, y, x),
    )
    neighbours = receivers + (mate,)
    y_pair, y_cross = y + 1 - 2 * yl, y - 1 + 2 * yl + 4
    f_peers = [(me_d, (me_f + k) % 16) for k in range(1, 16)]
    d_peers = [((me_d + k) % 16, me_f) for k in range(1, 16)]

    barrier = pltpu.get_barrier_semaphore()
    for peer in neighbours:
        pl.semaphore_signal(barrier, inc=1, device_id=peer, device_id_type=MESH)

    def hidden_copy(g):
        return pltpu.make_async_copy(
            hid_ref.at[:, pl.ds(pl.multiple_of(g * GROUP, GROUP), GROUP)], hbuf.at[g], hsem.at[g]
        )

    def start_hidden(g, carry):
        hidden_copy(g).start()
        return carry

    lax.fori_loop(0, 32, start_hidden, 0)
    local = [
        pltpu.make_async_copy(src, dst, lsem.at[i])
        for i, (src, dst) in enumerate((
            (w_ref, wbuf.at[chip]), (ad_hbm, ad_ref), (og_hbm, og_ref), (len_hbm, len_ref), (assign_hbm, assign_ref),
            (adv_hbm, adv_ref), (gain_hbm, gain_ref), (bias_hbm, bias_ref), (up_hbm, up_ref),
        ))
    ]
    for copy in local:
        copy.start()
    ssq[...] = jnp.zeros_like(ssq)
    low2[...] = jnp.zeros_like(low2)

    pl.semaphore_wait(barrier, 7)

    def send_tokens(i):
        for peer in neighbours:
            pl.semaphore_signal(tokens.at[i], inc=1, device_id=peer, device_id_type=MESH)

    def take_tokens(i):
        pl.semaphore_wait(tokens.at[i], 7)

    def shard(dx, dy):
        return (yl + dy - 2 * yl * dy) * 4 + (x + dx) % 4

    def rows_of(v):
        k = v + par if v % 2 == 0 else v - par
        return pl.ds(pl.multiple_of(k * PIECE, PIECE), PIECE)

    def piece_send(e):
        _, link, dx, dy, v = ENTRIES[e]
        sx, sy, sv = source_of(link, dx, dy, v)
        f, rows = shard(sx, sy), rows_of(sv)
        own = (sx, sy) == (0, 0)
        return pltpu.make_async_remote_copy(
            src_ref=w_ref.at[rows] if own else wbuf.at[f, rows],
            dst_ref=wbuf.at[f, rows],
            send_sem=wsend.at[e], recv_sem=wrecv.at[e],
            device_id=receivers[link], device_id_type=MESH,
        )

    def piece_landing(e):
        _, link, dx, dy, v = ENTRIES[e]
        spot = wbuf.at[shard(dx, dy), rows_of(v)]
        return pltpu.make_async_remote_copy(
            src_ref=spot, dst_ref=spot, send_sem=wsend.at[e], recv_sem=wrecv.at[e],
            device_id=mate, device_id_type=MESH,
        )

    def pass_on(i, v):
        dx, dy, h = LATE[i]
        k = v + par if v % 2 == 0 else v - par
        return pltpu.make_async_remote_copy(
            src_ref=wbuf.at[shard(dx, dy), rows_of(v)],
            dst_ref=wlate.at[i, pl.ds(pl.multiple_of((k - 4 * h) * PIECE, PIECE), PIECE)],
            send_sem=psend.at[4 * i + v - 4 * h], recv_sem=precv.at[4 * i + v - 4 * h],
            device_id=mate, device_id_type=MESH,
        )

    def multiply_late(i):
        dx, dy, h = LATE[i]
        g = (2 * shard(dx, dy) + 1 - c) * 2 + h
        acc[:256, :] += jnp.dot(nbuf[g, :256, :], wlate[i], preferred_element_type=jnp.float32)

    def multiply(items, rows):
        def body(i, carry):
            j = shard(lookup(i, [item[0] for item in items]), lookup(i, [item[1] for item in items]))
            h = lookup(i, [item[2] for item in items])
            span = pl.ds(pl.multiple_of(h * GROUP, GROUP), GROUP)
            acc[rows, :] += jnp.dot(
                nbuf[(2 * j + c) * 2 + h, rows, :], wbuf[j, span, :], preferred_element_type=jnp.float32
            )
            return carry

        lax.fori_loop(0, len(items), body, 0)

    def sum_squares(g, carry):
        hidden_copy(g).wait()
        wide = hbuf[g].astype(jnp.float32)
        squared = wide * wide
        ssq[...] += squared[:, :128] + squared[:, 128:]
        return carry

    def scale_group(g, carry):
        gain = gain_ref[:, pl.ds(pl.multiple_of(g * GROUP, GROUP), GROUP)]
        nbuf[g, :256, :] = (hbuf[g].astype(jnp.float32) * ssq[:, :1] * gain).astype(jnp.bfloat16)
        return carry

    def lora_group(g, carry):
        cols = pl.ds(pl.multiple_of(g * GROUP, GROUP), GROUP)
        low2[...] += lax.dot_general(nbuf[g, :256, :], ad_ref[:, cols], NT, preferred_element_type=jnp.float32)
        return carry

    flag_copies = [
        pltpu.make_async_remote_copy(
            src_ref=flags.at[me_d], dst_ref=flags.at[me_d], send_sem=fsem.at[k], recv_sem=frecv.at[k],
            device_id=d_peers[k], device_id_type=MESH,
        )
        for k in range(15)
    ]
    def norm_copy(i):
        if i < 8:
            place = pl.ds((2 * i + 1 - c) * 2, 2)
        else:
            place = pl.ds((2 * (i - 8) + c) * 2 + 1 - c, 1)
        return pltpu.make_async_remote_copy(
            src_ref=nbuf.at[place, pl.ds(0, 256)], dst_ref=nbuf.at[place, pl.ds(256, 256)],
            send_sem=msem.at[0, i], recv_sem=msem.at[1, i], device_id=mate, device_id_type=MESH,
        )

    def part_copy(half):
        rows = pl.ds(half * 128, 128)
        return pltpu.make_async_remote_copy(
            src_ref=acc.at[pl.ds(256 + half * 128, 128)], dst_ref=part_acc.at[rows],
            send_sem=msem.at[0, 17 + half], recv_sem=msem.at[1, 17 + half], device_id=mate, device_id_type=MESH,
        )

    by_step = [[e for e in range(N_ENTRIES) if ENTRIES[e][0] == t] for t in range(len(SCHEDULE))]
    ready = [(0, 0, 0), (0, 0, 1)]
    mine, others = slice(0, 256), slice(256, 512)
    n_steps = len(SCHEDULE) + GAP
    for t in range(n_steps):
        if t >= GAP:
            for e in by_step[t - GAP]:
                piece_landing(e).wait_recv()
                _, _, dx, dy, v = ENTRIES[e]
                if (dx, dy, v // 4) in LATE:
                    pass_on(LATE.index((dx, dy, v // 4)), v).start()
        for e in ISSUE[t]:
            piece_send(e).start()
        if 1 <= t <= 5:
            take_tokens(t - 1)
        if t < 5:
            send_tokens(t)
        for key, done in GROUP_DONE.items():
            if done == t - GAP and key not in LATE:
                ready.append(key)
        if t == 0:
            lax.fori_loop(0, 16, sum_squares, 0)
        if t == 1:
            lax.fori_loop(16, 32, sum_squares, 0)
            mean = jnp.sum(ssq[...], axis=1, keepdims=True) * (1.0 / 8192.0)
            ssq[...] = jnp.broadcast_to(lax.rsqrt(mean + EPSILON), ssq.shape)
            local[6].wait()
        if t == 2:
            lax.fori_loop(0, 16, scale_group, 0)
            for i in (0, 1, 2, 3, 8, 9, 10, 11):
                norm_copy(i).start()
        if t == 3:
            lax.fori_loop(16, 32, scale_group, 0)
            for i in (4, 5, 6, 7, 12, 13, 14, 15):
                norm_copy(i).start()
            local[1].wait()
        if t == 4:
            lax.fori_loop(0, 16, lora_group, 0)
        if t == 5:
            lax.fori_loop(16, 32, lora_group, 0)
            local[0].wait()
            local[7].wait()
            acc[mine, :] = jnp.broadcast_to(bias_ref[...].astype(jnp.float32).reshape(1, 768), (256, 768))
            acc[others, :] = jnp.zeros((256, 768), jnp.float32)
            for i in range(16):
                norm_copy(i).wait_recv()
        if t == 6:
            for i in (3, 4, 5, 8):
                local[i].wait()
            for r in range(8):
                flags[me_d, pl.ds(r, 1), :] = jnp.full((1, 128), assign_ref[r], jnp.int32)
            for copy in flag_copies:
                copy.start()
        if t >= 6 and ready:
            multiply(ready, slice(0, 512))
            ready = []
        if t == LATE_FROM - 1 + GAP:
            part_copy(0).start()
            part_copy(1).start()
    multiply(LATE, mine)
    for i in range(len(LATE)):
        for v in range(4 * LATE[i][2], 4 * LATE[i][2] + 4):
            pass_on(i, v).wait_recv()
        multiply_late(i)

    low = low2[...].astype(jnp.bfloat16)
    low_wide = jnp.concatenate([low, low], axis=1)
    lora = jnp.dot(low, up_ref[...], preferred_element_type=jnp.float32)
    row = lax.broadcasted_iota(jnp.int32, (128, 128), 0)
    col = lax.broadcasted_iota(jnp.int32, (128, 128), 1)
    same = (row // 32) == (col // 32)
    causal = same & ((col % 32) <= (row % 32))
    scale = 128 ** (-0.5)
    heads = [slice(h * 128, h * 128 + 128) for h in range(4)]

    def spread(ref, half, where, kind):
        out = jnp.full((128, 128), ref[half * 4].astype(kind), kind)
        for r in range(1, 4):
            out = jnp.where(where // 32 == r, jnp.full((128, 128), ref[half * 4 + r].astype(kind), kind), out)
        return out

    lives = [(row % 32) < spread(len_ref, half, row, jnp.int32) for half in range(2)]
    seen = [causal & ((col % 32) < spread(len_ref, half, col, jnp.int32)) for half in range(2)]
    for half in range(2):
        rows = slice(half * 128, half * 128 + 128)
        part_copy(half).wait_recv()
        projected = acc[rows, :] + part_acc[rows, :]
        queries = (projected[:, :512] + ADAPTER_SCALE * lora[rows, :]).astype(jnp.bfloat16)
        keys = projected[:, 512:640].astype(jnp.bfloat16)
        values = projected[:, 640:].astype(jnp.bfloat16)
        kbuf[rows, :] = keys
        vbuf[rows, :] = values
        scores = [lax.dot_general(queries[:, h], keys, NT, preferred_element_type=jnp.float32) for h in heads]
        scores = [jnp.where(seen[half], s * scale, jnp.float32(-1e30)) for s in scores]
        raised = [jnp.exp(s - jnp.max(s, axis=-1, keepdims=True)) for s in scores]
        soft = [r / jnp.sum(r, axis=-1, keepdims=True) for r in raised]
        outs = [jnp.dot(p.astype(jnp.bfloat16), values, preferred_element_type=jnp.float32) for p in soft]
        for i, h in enumerate(heads):
            pbuf[half * 4 + i] = soft[i]
            out = jnp.where(lives[half], outs[i], 0.0).astype(jnp.bfloat16)
            attb[half * 4 : half * 4 + 4, :, h] = out.reshape(4, 32, 128)

    def fill_slot(d, carry):
        which = jnp.int32(0)
        for r in range(1, 8):
            which = jnp.where(assign_ref[r] == d, jnp.int32(r), which)
        pay_s[d] = attb[which]
        return carry

    lax.fori_loop(0, 16, fill_slot, 0)
    rec_s[me_d] = pay_s[me_d]
    slot_copies = [
        pltpu.make_async_remote_copy(
            src_ref=pay_s.at[(me_d + ORDER[i]) % 16], dst_ref=rec_s.at[me_d], send_sem=ssem.at[i],
            recv_sem=srecv.at[i], device_id=((me_d + ORDER[i]) % 16, me_f), device_id_type=MESH,
        )
        for i in range(15)
    ]
    for copy in slot_copies[:SPLIT]:
        copy.start()

    local[2].wait()
    for half in range(2):
        rows = slice(half * 128, half * 128 + 128)
        factor = spread(adv_ref, half, row, jnp.float32) / spread(len_ref, half, row, jnp.float32)
        keys, values = kbuf[rows, :], vbuf[rows, :]
        weighted = [(og_ref[rows, h].astype(jnp.float32) * factor).astype(jnp.bfloat16) for h in heads]
        weighted = [jnp.where(lives[half], w.astype(jnp.float32), 0.0).astype(jnp.bfloat16) for w in weighted]
        dsoft = [lax.dot_general(w, values, NT, preferred_element_type=jnp.float32) for w in weighted]
        dsoft = [d.astype(jnp.bfloat16).astype(jnp.float32) for d in dsoft]
        soft = [pbuf[half * 4 + i] for i in range(4)]
        inner = [jnp.sum(d * p, axis=-1, keepdims=True) for d, p in zip(dsoft, soft)]
        dscores = [(p * (d - i) * scale).astype(jnp.bfloat16) for d, p, i in zip(dsoft, soft, inner)]
        dquery = [jnp.dot(d, keys, preferred_element_type=jnp.float32) for d in dscores]
        for d, h in zip(dquery, heads):
            qg[rows, h] = d.astype(jnp.bfloat16)
    low_grad = ADAPTER_SCALE * lax.dot_general(up_ref[...], qg[...], NT, preferred_element_type=jnp.float32)
    lg[:, :256] = low_grad.astype(jnp.bfloat16)
    lg_copy = pltpu.make_async_remote_copy(
        src_ref=lg.at[:, pl.ds(0, 256)], dst_ref=lg.at[:, pl.ds(256, 256)], send_sem=msem.at[0, 16], recv_sem=msem.at[1, 16],
        device_id=mate, device_id_type=MESH,
    )
    lg_copy.start()
    up_grad = ADAPTER_SCALE * lax.dot_general(qg[...], low_wide, TN, preferred_element_type=jnp.float32)
    up_four = up_grad.reshape(16, 2, 16, 128)
    lane = lax.broadcasted_iota(jnp.int32, (16, 16, 128), 2)
    ordered[...] = jnp.where(lane < 64, up_four[:, 0], up_four[:, 1]).astype(jnp.bfloat16)
    lg_copy.wait()

    def down_slice(i, carry):
        d = (z + lookup(i // 2, Z_ORDER)) % 8 * 2 + i % 2
        part = jnp.dot(lg[...], nbuf[2 * d + c], preferred_element_type=jnp.float32).astype(jnp.bfloat16)
        for i2 in range(4):
            for j2 in range(2):
                pay_a[j2 * 4 + i2, i] = part[i2 * 16 : i2 * 16 + 16, j2 * 128 : j2 * 128 + 128]
        return carry

    def a_copy(q, k):
        span = pl.ds(q * CHUNK, CHUNK)
        there = (chip + k) % 8
        other = (there // 4 + yl) % 2
        y_to = y + other * ((y_cross if q % 2 else y_pair) - y)
        return pltpu.make_async_remote_copy(
            src_ref=pay_a.at[there, span], dst_ref=rec_a.at[k - 1, span], send_sem=asem.at[q, k - 1],
            recv_sem=arecv.at[q, k - 1], device_id=at(z, y_to, there % 4), device_id_type=MESH,
        )

    chunks = range(16 // CHUNK)
    for q in chunks:
        lax.fori_loop(q * CHUNK, (q + 1) * CHUNK, down_slice, 0)
        for k in range(1, 8):
            a_copy(q, k).start()
    for e in range(N_ENTRIES):
        piece_send(e).wait_send()
    for i in range(16):
        norm_copy(i).wait_send()
    for half in range(2):
        part_copy(half).wait_send()
    for i in range(len(LATE)):
        for v in range(4 * LATE[i][2], 4 * LATE[i][2] + 4):
            pass_on(i, v).wait_send()
    for copy in flag_copies:
        copy.wait()
    def slice_at(i):
        return (z + Z_ORDER[i // 2]) % 8 * 2 + i % 2

    def b_copy(i):
        slot = i - i % 2 + yh if i < 14 else 14
        return pltpu.make_async_remote_copy(
            src_ref=pay_b.at[i if i < 14 else 15 - yh], dst_ref=rec_b.at[slot], send_sem=bsem.at[i],
            recv_sem=brecv.at[slot], device_id=(slice_at(i) if i < 14 else 2 * z + 1 - yh, me_f), device_id_type=MESH,
        )

    def b_landing(slot):
        return pltpu.make_async_remote_copy(
            src_ref=rec_b.at[slot], dst_ref=rec_b.at[slot], send_sem=bsem.at[slot], recv_sem=brecv.at[slot],
            device_id=mate, device_id_type=MESH,
        )

    for q in chunks:
        span = pl.ds(q * CHUNK, CHUNK)
        for k in range(1, 8):
            a_copy(q, k).wait()
        total = pay_a[chip, span].astype(jnp.float32)
        for k in range(7):
            total += rec_a[k, span].astype(jnp.float32)
        pay_b[span, 0] = total.astype(jnp.bfloat16)
        for i in range(q * CHUNK, (q + 1) * CHUNK):
            pay_b[i, 1] = ordered[slice_at(i)]
            if i < 14:
                b_copy(i).start()
    b_copy(14).start()

    for copy in slot_copies[SPLIT:]:
        copy.start()
    for i in range(15):
        b_copy(i).wait_send()
        b_landing(i).wait_recv()
    total = pay_b[14 + yh].astype(jnp.float32)
    for k in range(15):
        total += rec_b[k].astype(jnp.float32)
    pay_c[...] = total.astype(jnp.bfloat16)
    c_copies = [
        pltpu.make_async_remote_copy(
            src_ref=pay_c, dst_ref=rec_c.at[me_f], send_sem=gsem.at[k], recv_sem=grecv.at[k],
            device_id=f_peers[k], device_id_type=MESH,
        )
        for k in range(15)
    ]
    for copy in c_copies:
        copy.start()
    own_copy = pltpu.make_async_copy(pay_c, rec_c.at[me_f], lsem.at[10])
    own_copy.start()
    for copy in slot_copies:
        copy.wait()
    held = [jnp.sum((flags[s] == me_d).astype(jnp.float32), axis=0, keepdims=True) for s in range(16)]
    before = [jnp.zeros((1, 128), jnp.float32)]
    for s in range(15):
        before.append(before[-1] + held[s])
    for i in range(8):
        picked = jnp.zeros((32, 512), jnp.bfloat16)
        for s in range(i, i + 9):
            take = jnp.where(before[s] == float(i), held[s], 0.0).astype(jnp.bfloat16)
            picked += rec_s[s] * jnp.concatenate([take] * 4, axis=1)
        attb[i] = picked
    att_copy = pltpu.make_async_copy(attb, att_out, lsem.at[9])
    att_copy.start()

    for copy in c_copies:
        copy.wait()
    own_copy.wait()
    att_copy.wait()


def assemble(att_ref, sums_ref, att_out, down_out, up_out):
    att_out[...] = att_ref[...]
    for f in range(16):
        j, i, core = f // 8, (f // 2) % 4, f % 2
        down_out[i * 16 : i * 16 + 16, core * 256 + j * 128 : core * 256 + j * 128 + 128] = sums_ref[f, 0].astype(
            jnp.float32
        )
    total = sums_ref[0, 1].astype(jnp.float32)
    for f in range(1, 16):
        total += sums_ref[f, 1].astype(jnp.float32)
    up_out[:16, :] = total[:, :64]
    up_out[16:, :] = total[:, 64:]


def on_device(
    hidden_input, input_norm_gain, joined_weight, joined_bias, adapter_down, adapter_up, advantage,
    output_gradient, lengths, assignment,
):
    bf16, f32 = jnp.bfloat16, jnp.float32
    dma = pltpu.SemaphoreType.DMA
    vmem = pl.BlockSpec(memory_space=pltpu.VMEM)
    hbm = pl.BlockSpec(memory_space=pl.ANY)
    att, sums = pl.pallas_call(
        kernel,
        out_shape=(jax.ShapeDtypeStruct((8, 32, 512), bf16), jax.ShapeDtypeStruct((16, 2, 16, 128), bf16)),
        in_specs=[hbm] * 10,
        out_specs=(hbm, hbm),
        scratch_shapes=[
            pltpu.SMEM((8,), jnp.int32),
            pltpu.SMEM((8,), jnp.int32),
            pltpu.SMEM((8,), f32),
            pltpu.VMEM((1, 8192), f32),
            pltpu.VMEM((768,), bf16),
            pltpu.VMEM((64, 8192), bf16),
            pltpu.VMEM((64, 512), bf16),
            pltpu.VMEM((256, 512), bf16),
            pltpu.VMEM((32, 256, 256), bf16),
            pltpu.VMEM((32, 512, 256), bf16),
            pltpu.VMEM((8, 512, 768), bf16),
            pltpu.VMEM((len(LATE), 256, 768), bf16),
            pltpu.VMEM((512, 768), f32),
            pltpu.VMEM((256, 768), f32),
            pltpu.VMEM((256, 128), f32),
            pltpu.VMEM((256, 128), bf16),
            pltpu.VMEM((256, 128), bf16),
            pltpu.VMEM((256, 64), f32),
            pltpu.VMEM((8, 32, 512), bf16),
            pltpu.VMEM((8, 128, 128), f32),
            pltpu.VMEM((256, 512), bf16),
            pltpu.VMEM((64, 512), bf16),
            pltpu.VMEM((16, 8, 128), jnp.int32),
            pltpu.VMEM((16, 32, 512), bf16),
            pltpu.VMEM((16, 32, 512), bf16),
            pltpu.VMEM((16, 16, 128), bf16),
            pltpu.VMEM((8, 16, 16, 128), bf16),
            pltpu.VMEM((7, 16, 16, 128), bf16),
            pltpu.VMEM((16, 2, 16, 128), bf16),
            pltpu.VMEM((15, 2, 16, 128), bf16),
            pltpu.VMEM((2, 16, 128), bf16),
            pltpu.SemaphoreType.REGULAR((5,)),
            dma((32,)), dma((11,)), dma((N_ENTRIES,)), dma((N_ENTRIES,)), dma((4 * len(LATE),)), dma((4 * len(LATE),)),
            dma((2, 19)), dma((15,)), dma((15,)), dma((15,)), dma((15,)), dma((16 // CHUNK, 7)), dma((16 // CHUNK, 7)),
            dma((15,)), dma((15,)), dma((15,)), dma((15,)),
        ],
        compiler_params=pltpu.CompilerParams(
            collective_id=0, has_side_effects=True, vmem_limit_bytes=56 * 2**20
        ),
        name="block",
    )(
        lengths,
        assignment,
        advantage,
        hidden_input.reshape(256, 8192),
        input_norm_gain.reshape(1, 8192),
        joined_weight,
        joined_bias,
        adapter_down.T,
        adapter_up,
        output_gradient.reshape(256, 512),
    )
    att, down, up = pl.pallas_call(
        assemble,
        out_shape=(
            jax.ShapeDtypeStruct((8, 32, 512), bf16),
            jax.ShapeDtypeStruct((64, 512), f32),
            jax.ShapeDtypeStruct((32, 64), f32),
        ),
        in_specs=[vmem, vmem],
        out_specs=(vmem, vmem, vmem),
        name="assemble",
    )(att, sums)
    return att, down.T, up.T


def solution(mesh):
    in_specs = (
        P(("dp", "fsdp"), None, None),
        P(),
        P("fsdp", None),
        P(),
        P(),
        P(),
        P(("dp", "fsdp")),
        P(("dp", "fsdp"), None, None),
        P(("dp", "fsdp")),
        P(("dp", "fsdp")),
    )
    out_specs = (P(("dp", "fsdp"), None, None), P("dp", None), P(None, "dp"))
    return jax.shard_map(
        on_device, mesh=mesh, in_specs=in_specs, out_specs=out_specs, check_vma=False
    )
```

```python
import jax
import jax.numpy as jnp
from jax import lax
from jax.experimental import pallas as pl
from jax.experimental.pallas import tpu as pltpu
from jax.sharding import PartitionSpec as P

EPSILON = 1e-06
ADAPTER_SCALE = 2.0
MESH = pl.DeviceIdType.MESH
NT = (((1,), (1,)), ((), ()))
TN = (((0,), (0,)), ((), ()))

SCHEDULE = (
    ((0, 1, 0, 4), (1, 3, 0, 0), (2, 0, 1, 4), (3, 0, 1, 6)),
    ((0, 1, 0, 0), (1, 3, 0, 4), (2, 0, 1, 0), (3, 0, 1, 2)),
    ((0, 1, 0, 2), (1, 3, 0, 6), (2, 0, 1, 5), (3, 0, 1, 1)),
    ((0, 1, 1, 6), (1, 3, 0, 2), (2, 1, 1, 4), (3, 3, 1, 0), (4, 1, 0, 5), (5, 3, 0, 1)),
    ((0, 1, 0, 6), (1, 3, 1, 2), (2, 1, 1, 0), (3, 0, 1, 7), (4, 1, 0, 1), (5, 3, 0, 5)),
    ((0, 2, 0, 4), (1, 2, 0, 0), (2, 1, 1, 2), (3, 3, 1, 6), (4, 3, 0, 7), (5, 1, 0, 3)),
    ((0, 2, 1, 4), (1, 2, 0, 2), (2, 0, 1, 3), (3, 3, 1, 4), (4, 3, 1, 1), (5, 1, 1, 7)),
    ((0, 1, 0, 7), (1, 2, 0, 6), (2, 1, 1, 5), (3, 1, 1, 1), (4, 3, 0, 3), (5, 3, 1, 3)),
    ((0, 2, 1, 6), (1, 2, 1, 2), (2, 3, 1, 7), (3, 2, 1, 0), (4, 2, 0, 5), (5, 2, 0, 1)),
    ((0, 2, 1, 7), (1, 2, 0, 7), (2, 1, 1, 3), (3, 3, 1, 5), (4, 2, 0, 3), (5, 2, 1, 5)),
    ((0, 2, 1, 1), (1, 2, 1, 3)),
)
ENTRIES = tuple((t,) + e for t, row in enumerate(SCHEDULE) for e in row)
N_ENTRIES = len(ENTRIES)
GAP = 3
PIECE = 64
ORDER = (7, 8, 9, 10, 6, 5, 11, 12, 4, 3, 13, 14, 2, 1, 15)
Z_ORDER = (4, 3, 5, 2, 6, 1, 7, 0)
CHUNK = 4
GROUP = 256


def source_of(link, dx, dy, v):
    if link == 0:
        return (dx + 3) % 4, dy, v
    if link == 1:
        return (dx + 1) % 4, dy, v
    if link < 4:
        return dx, 1 - dy, v
    return dx, dy, v ^ 1


def group_plan():
    done = {}
    for t, _, dx, dy, v in ENTRIES:
        key = (dx, dy, v // 4)
        done[key] = max(done.get(key, 0), t)
    return done


GROUP_DONE = group_plan()
AHEAD = 1
LATE_FROM = len(SCHEDULE) - 1
LATE = tuple(key for key in GROUP_DONE if GROUP_DONE[key] >= LATE_FROM)
SPLIT = 6


def issue_plan():
    slot_of = {(dx, dy, v): t for t, _, dx, dy, v in ENTRIES}
    plan = [[] for _ in range(len(SCHEDULE) + GAP)]
    latest = {}
    for e, (t, link, dx, dy, v) in enumerate(ENTRIES):
        sx, sy, sv = source_of(link, dx, dy, v)
        have = 0 if (sx, sy) == (0, 0) else slot_of[sx, sy, sv] + GAP
        latest[link] = max(have, t - AHEAD, latest.get(link, 0))
        plan[latest[link]].append(e)
    return plan


ISSUE = issue_plan()


def lookup(index, values):
    out = jnp.int32(values[0])
    for i in range(1, len(values)):
        out = jnp.where(index == i, jnp.int32(values[i]), out)
    return out


def kernel(
    len_hbm, assign_hbm, adv_hbm, hid_ref, gain_hbm, w_ref, bias_hbm, ad_hbm, up_hbm, og_hbm,
    att_out, rec_c,
    len_ref, assign_ref, adv_ref, gain_ref, bias_ref, ad_ref, up_ref, og_ref,
    hbuf, nbuf, wbuf, wlate, acc, part_acc, ssq, kbuf, vbuf, low2, attb, pbuf, qg, lg,
    flags, pay_s, rec_s, ordered, pay_a, rec_a, pay_b, rec_b, pay_c,
    tokens, hsem, lsem, wsend, wrecv, psend, precv, msem, fsem, frecv, ssem, srecv, asem, arecv, bsem,
    brecv, gsem, grecv,
):
    me_d, me_f = lax.axis_index("dp"), lax.axis_index("fsdp")
    z, yh = me_d // 2, me_d % 2
    yl, x, c = me_f // 8, (me_f // 2) % 4, me_f % 2
    y = yh * 2 + yl
    par = z % 2
    chip = me_f // 2
    mate_f = me_f + 1 - 2 * c
    mate = (me_d, mate_f)

    def at(z_, y_, x_):
        return ((z_ % 8) * 2 + (y_ % 4) // 2, ((y_ % 4) % 2) * 8 + (x_ % 4) * 2 + c)

    receivers = (
        at(z, y, x + 3), at(z, y, x + 1), at(z, y + 3, x), at(z, y + 1, x), at(z + 7, y, x), at(z + 1, y, x),
    )
    neighbours = receivers + (mate,)
    y_pair, y_cross = y + 1 - 2 * yl, y - 1 + 2 * yl + 4
    f_peers = [(me_d, (me_f + k) % 16) for k in (4, 12, 5, 3, 11, 13, 2, 14, 6, 10, 7, 9, 8, 15, 1)]
    d_peers = [((me_d + k) % 16, me_f) for k in range(1, 16)]

    barrier = pltpu.get_barrier_semaphore()
    for peer in neighbours:
        pl.semaphore_signal(barrier, inc=1, device_id=peer, device_id_type=MESH)

    local = [
        pltpu.make_async_copy(src, dst, lsem.at[i])
        for i, (src, dst) in enumerate((
            (w_ref, wbuf.at[chip]), (ad_hbm, ad_ref), (og_hbm, og_ref), (len_hbm, len_ref), (assign_hbm, assign_ref),
            (adv_hbm, adv_ref), (gain_hbm, gain_ref), (bias_hbm, bias_ref), (up_hbm, up_ref),
        ))
    ]
    pl.semaphore_wait(barrier, 7)

    def hidden_copy(g):
        return pltpu.make_async_copy(
            hid_ref.at[:, pl.ds(pl.multiple_of(g * GROUP, GROUP), GROUP)], hbuf.at[g], hsem.at[g]
        )

    def start_hidden(g, carry):
        hidden_copy(g).start()
        return carry

    def send_tokens(i):
        for peer in neighbours:
            pl.semaphore_signal(tokens.at[i], inc=1, device_id=peer, device_id_type=MESH)

    def take_tokens(i):
        pl.semaphore_wait(tokens.at[i], 7)

    def shard(dx, dy):
        return (yl + dy - 2 * yl * dy) * 4 + (x + dx) % 4

    def rows_of(v):
        k = v + par if v % 2 == 0 else v - par
        return pl.ds(pl.multiple_of(k * PIECE, PIECE), PIECE)

    def piece_send(e):
        _, link, dx, dy, v = ENTRIES[e]
        sx, sy, sv = source_of(link, dx, dy, v)
        f, rows = shard(sx, sy), rows_of(sv)
        own = (sx, sy) == (0, 0)
        return pltpu.make_async_remote_copy(
            src_ref=w_ref.at[rows] if own else wbuf.at[f, rows],
            dst_ref=wbuf.at[f, rows],
            send_sem=wsend.at[e], recv_sem=wrecv.at[e],
            device_id=receivers[link], device_id_type=MESH,
        )

    def piece_landing(e):
        _, link, dx, dy, v = ENTRIES[e]
        spot = wbuf.at[shard(dx, dy), rows_of(v)]
        return pltpu.make_async_remote_copy(
            src_ref=spot, dst_ref=spot, send_sem=wsend.at[e], recv_sem=wrecv.at[e],
            device_id=mate, device_id_type=MESH,
        )

    def pass_on(i, v):
        dx, dy, h = LATE[i]
        k = v + par if v % 2 == 0 else v - par
        return pltpu.make_async_remote_copy(
            src_ref=wbuf.at[shard(dx, dy), rows_of(v)],
            dst_ref=wlate.at[i, pl.ds(pl.multiple_of((k - 4 * h) * PIECE, PIECE), PIECE)],
            send_sem=psend.at[4 * i + v - 4 * h], recv_sem=precv.at[4 * i + v - 4 * h],
            device_id=mate, device_id_type=MESH,
        )

    def multiply_late(i):
        dx, dy, h = LATE[i]
        g = (2 * shard(dx, dy) + 1 - c) * 2 + h
        acc[:256, :] += jnp.dot(nbuf[g, :256, :], wlate[i], preferred_element_type=jnp.float32)

    def multiply(items, rows):
        def body(i, carry):
            j = shard(lookup(i, [item[0] for item in items]), lookup(i, [item[1] for item in items]))
            h = lookup(i, [item[2] for item in items])
            span = pl.ds(pl.multiple_of(h * GROUP, GROUP), GROUP)
            acc[rows, :] += jnp.dot(
                nbuf[(2 * j + c) * 2 + h, rows, :], wbuf[j, span, :], preferred_element_type=jnp.float32
            )
            return carry

        lax.fori_loop(0, len(items), body, 0)

    def sum_squares(g, carry):
        hidden_copy(g).wait()
        wide = hbuf[g].astype(jnp.float32)
        squared = wide * wide
        ssq[...] += squared[:, :128] + squared[:, 128:]
        return carry

    def scale_group(g, carry):
        gain = gain_ref[:, pl.ds(pl.multiple_of(g * GROUP, GROUP), GROUP)]
        nbuf[g, :256, :] = (hbuf[g].astype(jnp.float32) * ssq[:, :1] * gain).astype(jnp.bfloat16)
        return carry

    def lora_group(g, carry):
        cols = pl.ds(pl.multiple_of(g * GROUP, GROUP), GROUP)
        low2[...] += lax.dot_general(nbuf[g, :256, :], ad_ref[:, cols], NT, preferred_element_type=jnp.float32)
        return carry

    flag_copies = [
        pltpu.make_async_remote_copy(
            src_ref=flags.at[me_d], dst_ref=flags.at[me_d], send_sem=fsem.at[k], recv_sem=frecv.at[k],
            device_id=d_peers[k], device_id_type=MESH,
        )
        for k in range(15)
    ]
    def norm_copy(i):
        if i < 8:
            place = pl.ds((2 * i + 1 - c) * 2, 2)
        else:
            place = pl.ds((2 * (i - 8) + c) * 2 + 1 - c, 1)
        return pltpu.make_async_remote_copy(
            src_ref=nbuf.at[place, pl.ds(0, 256)], dst_ref=nbuf.at[place, pl.ds(256, 256)],
            send_sem=msem.at[0, i], recv_sem=msem.at[1, i], device_id=mate, device_id_type=MESH,
        )

    def part_copy(half):
        rows = pl.ds(half * 128, 128)
        return pltpu.make_async_remote_copy(
            src_ref=acc.at[pl.ds(256 + half * 128, 128)], dst_ref=part_acc.at[rows],
            send_sem=msem.at[0, 17 + half], recv_sem=msem.at[1, 17 + half], device_id=mate, device_id_type=MESH,
        )

    by_step = [[e for e in range(N_ENTRIES) if ENTRIES[e][0] == t] for t in range(len(SCHEDULE))]
    ready = [(0, 0, 0), (0, 0, 1)]
    mine, others = slice(0, 256), slice(256, 512)
    n_steps = len(SCHEDULE) + GAP
    for t in range(n_steps):
        if t >= GAP:
            for e in by_step[t - GAP]:
                piece_landing(e).wait_recv()
                _, _, dx, dy, v = ENTRIES[e]
                if (dx, dy, v // 4) in LATE:
                    pass_on(LATE.index((dx, dy, v // 4)), v).start()
        for e in ISSUE[t]:
            piece_send(e).start()
        if 1 <= t <= 5:
            take_tokens(t - 1)
        if t < 5:
            send_tokens(t)
        for key, done in GROUP_DONE.items():
            if done == t - GAP and key not in LATE:
                ready.append(key)
        if t == 0:
            lax.fori_loop(0, 32, start_hidden, 0)
            for copy in local:
                copy.start()
            ssq[...] = jnp.zeros_like(ssq)
            low2[...] = jnp.zeros_like(low2)
            lax.fori_loop(0, 16, sum_squares, 0)
        if t == 1:
            lax.fori_loop(16, 32, sum_squares, 0)
            mean = jnp.sum(ssq[...], axis=1, keepdims=True) * (1.0 / 8192.0)
            ssq[...] = jnp.broadcast_to(lax.rsqrt(mean + EPSILON), ssq.shape)
            local[6].wait()
        if t == 2:
            lax.fori_loop(0, 16, scale_group, 0)
            for i in (0, 1, 2, 3, 8, 9, 10, 11):
                norm_copy(i).start()
        if t == 3:
            lax.fori_loop(16, 32, scale_group, 0)
            for i in (4, 5, 6, 7, 12, 13, 14, 15):
                norm_copy(i).start()
            local[1].wait()
        if t == 4:
            lax.fori_loop(0, 16, lora_group, 0)
        if t == 5:
            lax.fori_loop(16, 32, lora_group, 0)
            local[0].wait()
            local[7].wait()
            acc[mine, :] = jnp.broadcast_to(bias_ref[...].astype(jnp.float32).reshape(1, 768), (256, 768))
            acc[others, :] = jnp.zeros((256, 768), jnp.float32)
            for i in range(16):
                norm_copy(i).wait_recv()
        if t == 6:
            for i in (3, 4, 5, 8):
                local[i].wait()
            for r in range(8):
                flags[me_d, pl.ds(r, 1), :] = jnp.full((1, 128), assign_ref[r], jnp.int32)
            for copy in flag_copies:
                copy.start()
        if t >= 6 and ready:
            multiply(ready, slice(0, 512))
            ready = []
        if t == LATE_FROM - 1 + GAP:
            part_copy(0).start()
            part_copy(1).start()
    multiply(LATE, mine)
    for i in range(len(LATE)):
        for v in range(4 * LATE[i][2], 4 * LATE[i][2] + 4):
            pass_on(i, v).wait_recv()
        multiply_late(i)

    low = low2[...].astype(jnp.bfloat16)
    low_wide = jnp.concatenate([low, low], axis=1)
    lora = jnp.dot(low, up_ref[...], preferred_element_type=jnp.float32)
    row = lax.broadcasted_iota(jnp.int32, (128, 128), 0)
    col = lax.broadcasted_iota(jnp.int32, (128, 128), 1)
    same = (row // 32) == (col // 32)
    causal = same & ((col % 32) <= (row % 32))
    scale = 128 ** (-0.5)
    heads = [slice(h * 128, h * 128 + 128) for h in range(4)]

    def spread(ref, half, where, kind):
        out = jnp.full((128, 128), ref[half * 4].astype(kind), kind)
        for r in range(1, 4):
            out = jnp.where(where // 32 == r, jnp.full((128, 128), ref[half * 4 + r].astype(kind), kind), out)
        return out

    lives = [(row % 32) < spread(len_ref, half, row, jnp.int32) for half in range(2)]
    seen = [causal & ((col % 32) < spread(len_ref, half, col, jnp.int32)) for half in range(2)]
    for half in range(2):
        rows = slice(half * 128, half * 128 + 128)
        part_copy(half).wait_recv()
        projected = acc[rows, :] + part_acc[rows, :]
        queries = (projected[:, :512] + ADAPTER_SCALE * lora[rows, :]).astype(jnp.bfloat16)
        keys = projected[:, 512:640].astype(jnp.bfloat16)
        values = projected[:, 640:].astype(jnp.bfloat16)
        kbuf[rows, :] = keys
        vbuf[rows, :] = values
        scores = [lax.dot_general(queries[:, h], keys, NT, preferred_element_type=jnp.float32) for h in heads]
        scores = [jnp.where(seen[half], s * scale, jnp.float32(-1e30)) for s in scores]
        raised = [jnp.exp(s - jnp.max(s, axis=-1, keepdims=True)) for s in scores]
        soft = [r / jnp.sum(r, axis=-1, keepdims=True) for r in raised]
        outs = [jnp.dot(p.astype(jnp.bfloat16), values, preferred_element_type=jnp.float32) for p in soft]
        for i, h in enumerate(heads):
            pbuf[half * 4 + i] = soft[i]
            out = jnp.where(lives[half], outs[i], 0.0).astype(jnp.bfloat16)
            attb[half * 4 : half * 4 + 4, :, h] = out.reshape(4, 32, 128)

    def fill_slot(d, carry):
        which = jnp.int32(0)
        for r in range(1, 8):
            which = jnp.where(assign_ref[r] == d, jnp.int32(r), which)
        pay_s[d] = attb[which]
        return carry

    lax.fori_loop(0, 16, fill_slot, 0)
    rec_s[me_d] = pay_s[me_d]
    slot_copies = [
        pltpu.make_async_remote_copy(
            src_ref=pay_s.at[(me_d + ORDER[i]) % 16], dst_ref=rec_s.at[me_d], send_sem=ssem.at[i],
            recv_sem=srecv.at[i], device_id=((me_d + ORDER[i]) % 16, me_f), device_id_type=MESH,
        )
        for i in range(15)
    ]
    for copy in slot_copies[:SPLIT]:
        copy.start()

    local[2].wait()
    for half in range(2):
        rows = slice(half * 128, half * 128 + 128)
        factor = spread(adv_ref, half, row, jnp.float32) / spread(len_ref, half, row, jnp.float32)
        keys, values = kbuf[rows, :], vbuf[rows, :]
        weighted = [(og_ref[rows, h].astype(jnp.float32) * factor).astype(jnp.bfloat16) for h in heads]
        weighted = [jnp.where(lives[half], w.astype(jnp.float32), 0.0).astype(jnp.bfloat16) for w in weighted]
        dsoft = [lax.dot_general(w, values, NT, preferred_element_type=jnp.float32) for w in weighted]
        dsoft = [d.astype(jnp.bfloat16).astype(jnp.float32) for d in dsoft]
        soft = [pbuf[half * 4 + i] for i in range(4)]
        inner = [jnp.sum(d * p, axis=-1, keepdims=True) for d, p in zip(dsoft, soft)]
        dscores = [(p * (d - i) * scale).astype(jnp.bfloat16) for d, p, i in zip(dsoft, soft, inner)]
        dquery = [jnp.dot(d, keys, preferred_element_type=jnp.float32) for d in dscores]
        for d, h in zip(dquery, heads):
            qg[rows, h] = d.astype(jnp.bfloat16)
    low_grad = ADAPTER_SCALE * lax.dot_general(up_ref[...], qg[...], NT, preferred_element_type=jnp.float32)
    lg[:, :256] = low_grad.astype(jnp.bfloat16)
    lg_copy = pltpu.make_async_remote_copy(
        src_ref=lg.at[:, pl.ds(0, 256)], dst_ref=lg.at[:, pl.ds(256, 256)], send_sem=msem.at[0, 16], recv_sem=msem.at[1, 16],
        device_id=mate, device_id_type=MESH,
    )
    lg_copy.start()
    up_grad = ADAPTER_SCALE * lax.dot_general(qg[...], low_wide, TN, preferred_element_type=jnp.float32)
    up_four = up_grad.reshape(16, 2, 16, 128)
    lane = lax.broadcasted_iota(jnp.int32, (16, 16, 128), 2)
    ordered[...] = jnp.where(lane < 64, up_four[:, 0], up_four[:, 1]).astype(jnp.bfloat16)
    lg_copy.wait()

    def down_slice(i, carry):
        d = (z + lookup(i // 2, Z_ORDER)) % 8 * 2 + i % 2
        part = jnp.dot(lg[...], nbuf[2 * d + c], preferred_element_type=jnp.float32).astype(jnp.bfloat16)
        for i2 in range(4):
            for j2 in range(2):
                pay_a[j2 * 4 + i2, i] = part[i2 * 16 : i2 * 16 + 16, j2 * 128 : j2 * 128 + 128]
        return carry

    def a_copy(q, k):
        span = pl.ds(q * CHUNK, CHUNK)
        there = (chip + k) % 8
        other = (there // 4 + yl) % 2
        y_to = y + other * ((y_cross if q % 2 else y_pair) - y)
        return pltpu.make_async_remote_copy(
            src_ref=pay_a.at[there, span], dst_ref=rec_a.at[k - 1, span], send_sem=asem.at[q, k - 1],
            recv_sem=arecv.at[q, k - 1], device_id=at(z, y_to, there % 4), device_id_type=MESH,
        )

    chunks = range(16 // CHUNK)
    for q in chunks:
        lax.fori_loop(q * CHUNK, (q + 1) * CHUNK, down_slice, 0)
        for k in range(1, 8):
            a_copy(q, k).start()
    for e in range(N_ENTRIES):
        piece_send(e).wait_send()
    for i in range(16):
        norm_copy(i).wait_send()
    for half in range(2):
        part_copy(half).wait_send()
    for i in range(len(LATE)):
        for v in range(4 * LATE[i][2], 4 * LATE[i][2] + 4):
            pass_on(i, v).wait_send()
    for copy in flag_copies:
        copy.wait()
    def slice_at(i):
        return (z + Z_ORDER[i // 2]) % 8 * 2 + i % 2

    def b_copy(i):
        slot = i - i % 2 + yh if i < 14 else 14
        return pltpu.make_async_remote_copy(
            src_ref=pay_b.at[i if i < 14 else 15 - yh], dst_ref=rec_b.at[slot], send_sem=bsem.at[i],
            recv_sem=brecv.at[0], device_id=(slice_at(i) if i < 14 else 2 * z + 1 - yh, me_f), device_id_type=MESH,
        )

    for q in chunks:
        span = pl.ds(q * CHUNK, CHUNK)
        for k in range(1, 8):
            a_copy(q, k).wait()
        total = pay_a[chip, span].astype(jnp.float32)
        for k in range(7):
            total += rec_a[k, span].astype(jnp.float32)
        pay_b[span, 0] = total.astype(jnp.bfloat16)
        for i in range(q * CHUNK, (q + 1) * CHUNK):
            pay_b[i, 1] = ordered[slice_at(i)]
            if i < 14:
                b_copy(i).start()
    b_copy(14).start()

    for copy in slot_copies[SPLIT:]:
        copy.start()
    pltpu.make_async_copy(rec_b, rec_b, brecv.at[0]).wait()
    total = pay_b[14 + yh].astype(jnp.float32)
    for k in range(15):
        total += rec_b[k].astype(jnp.float32)
    pay_c[...] = total.astype(jnp.bfloat16)
    c_copies = [
        pltpu.make_async_remote_copy(
            src_ref=pay_c, dst_ref=rec_c.at[me_f], send_sem=gsem.at[0], recv_sem=grecv.at[0],
            device_id=f_peers[k], device_id_type=MESH,
        )
        for k in range(15)
    ]
    for copy in c_copies:
        copy.start()
    own_copy = pltpu.make_async_copy(pay_c, rec_c.at[me_f], lsem.at[10])
    own_copy.start()
    for copy in slot_copies:
        copy.wait()
    held = [jnp.sum((flags[s] == me_d).astype(jnp.float32), axis=0, keepdims=True) for s in range(16)]
    before = [jnp.zeros((1, 128), jnp.float32)]
    for s in range(15):
        before.append(before[-1] + held[s])
    for i in range(8):
        picked = jnp.zeros((32, 512), jnp.bfloat16)
        for s in range(i, i + 9):
            take = jnp.where(before[s] == float(i), held[s], 0.0).astype(jnp.bfloat16)
            picked += rec_s[s] * jnp.concatenate([take] * 4, axis=1)
        attb[i] = picked
    att_copy = pltpu.make_async_copy(attb, att_out, lsem.at[9])
    att_copy.start()

    for i in range(15):
        b_copy(i).wait_send()
    most = rec_c.at[pl.ds(0, 15)]
    pltpu.make_async_copy(most, most, grecv.at[0]).wait()
    pltpu.make_async_copy(most, most, gsem.at[0]).wait()
    own_copy.wait()
    att_copy.wait()


def assemble(att_ref, sums_ref, att_out, down_out, up_out):
    att_out[...] = att_ref[...]
    for f in range(16):
        j, i, core = f // 8, (f // 2) % 4, f % 2
        down_out[i * 16 : i * 16 + 16, core * 256 + j * 128 : core * 256 + j * 128 + 128] = sums_ref[f, 0].astype(
            jnp.float32
        )
    total = sums_ref[0, 1].astype(jnp.float32)
    for f in range(1, 16):
        total += sums_ref[f, 1].astype(jnp.float32)
    up_out[:16, :] = total[:, :64]
    up_out[16:, :] = total[:, 64:]


def on_device(
    hidden_input, input_norm_gain, joined_weight, joined_bias, adapter_down, adapter_up, advantage,
    output_gradient, lengths, assignment,
):
    bf16, f32 = jnp.bfloat16, jnp.float32
    dma = pltpu.SemaphoreType.DMA
    vmem = pl.BlockSpec(memory_space=pltpu.VMEM)
    hbm = pl.BlockSpec(memory_space=pl.ANY)
    att, sums = pl.pallas_call(
        kernel,
        out_shape=(jax.ShapeDtypeStruct((8, 32, 512), bf16), jax.ShapeDtypeStruct((16, 2, 16, 128), bf16)),
        in_specs=[hbm] * 10,
        out_specs=(hbm, hbm),
        scratch_shapes=[
            pltpu.SMEM((8,), jnp.int32),
            pltpu.SMEM((8,), jnp.int32),
            pltpu.SMEM((8,), f32),
            pltpu.VMEM((1, 8192), f32),
            pltpu.VMEM((768,), bf16),
            pltpu.VMEM((64, 8192), bf16),
            pltpu.VMEM((64, 512), bf16),
            pltpu.VMEM((256, 512), bf16),
            pltpu.VMEM((32, 256, 256), bf16),
            pltpu.VMEM((32, 512, 256), bf16),
            pltpu.VMEM((8, 512, 768), bf16),
            pltpu.VMEM((len(LATE), 256, 768), bf16),
            pltpu.VMEM((512, 768), f32),
            pltpu.VMEM((256, 768), f32),
            pltpu.VMEM((256, 128), f32),
            pltpu.VMEM((256, 128), bf16),
            pltpu.VMEM((256, 128), bf16),
            pltpu.VMEM((256, 64), f32),
            pltpu.VMEM((8, 32, 512), bf16),
            pltpu.VMEM((8, 128, 128), f32),
            pltpu.VMEM((256, 512), bf16),
            pltpu.VMEM((64, 512), bf16),
            pltpu.VMEM((16, 8, 128), jnp.int32),
            pltpu.VMEM((16, 32, 512), bf16),
            pltpu.VMEM((16, 32, 512), bf16),
            pltpu.VMEM((16, 16, 128), bf16),
            pltpu.VMEM((8, 16, 16, 128), bf16),
            pltpu.VMEM((7, 16, 16, 128), bf16),
            pltpu.VMEM((16, 2, 16, 128), bf16),
            pltpu.VMEM((15, 2, 16, 128), bf16),
            pltpu.VMEM((2, 16, 128), bf16),
            pltpu.SemaphoreType.REGULAR((5,)),
            dma((32,)), dma((11,)), dma((N_ENTRIES,)), dma((N_ENTRIES,)), dma((4 * len(LATE),)), dma((4 * len(LATE),)),
            dma((2, 19)), dma((15,)), dma((15,)), dma((15,)), dma((15,)), dma((16 // CHUNK, 7)), dma((16 // CHUNK, 7)),
            dma((15,)), dma((1,)), dma((1,)), dma((1,)),
        ],
        compiler_params=pltpu.CompilerParams(
            collective_id=0, has_side_effects=True, vmem_limit_bytes=56 * 2**20
        ),
        name="block",
    )(
        lengths,
        assignment,
        advantage,
        hidden_input.reshape(256, 8192),
        input_norm_gain.reshape(1, 8192),
        joined_weight,
        joined_bias,
        adapter_down.T,
        adapter_up,
        output_gradient.reshape(256, 512),
    )
    att, down, up = pl.pallas_call(
        assemble,
        out_shape=(
            jax.ShapeDtypeStruct((8, 32, 512), bf16),
            jax.ShapeDtypeStruct((64, 512), f32),
            jax.ShapeDtypeStruct((32, 64), f32),
        ),
        in_specs=[vmem, vmem],
        out_specs=(vmem, vmem, vmem),
        name="assemble",
    )(att, sums)
    return att, down.T, up.T


def solution(mesh):
    in_specs = (
        P(("dp", "fsdp"), None, None),
        P(),
        P("fsdp", None),
        P(),
        P(),
        P(),
        P(("dp", "fsdp")),
        P(("dp", "fsdp"), None, None),
        P(("dp", "fsdp")),
        P(("dp", "fsdp")),
    )
    out_specs = (P(("dp", "fsdp"), None, None), P("dp", None), P(None, "dp"))
    return jax.shard_map(
        on_device, mesh=mesh, in_specs=in_specs, out_specs=out_specs, check_vma=False
    )
```

```python
import jax
import jax.numpy as jnp
from jax import lax
from jax.experimental import pallas as pl
from jax.experimental.pallas import tpu as pltpu
from jax.sharding import PartitionSpec as P

EPSILON = 1e-06
ADAPTER_SCALE = 2.0
MESH = pl.DeviceIdType.MESH
NT = (((1,), (1,)), ((), ()))
TN = (((0,), (0,)), ((), ()))

SCHEDULE = (
    ((0, 1, 0, 4), (1, 3, 0, 0), (2, 0, 1, 4), (3, 0, 1, 6)),
    ((0, 1, 0, 0), (1, 3, 0, 4), (2, 0, 1, 0), (3, 0, 1, 2)),
    ((0, 1, 0, 2), (1, 3, 0, 6), (2, 0, 1, 5), (3, 0, 1, 1)),
    ((0, 1, 1, 6), (1, 3, 0, 2), (2, 1, 1, 4), (3, 3, 1, 0), (4, 1, 0, 5), (5, 3, 0, 1)),
    ((0, 1, 0, 6), (1, 3, 1, 2), (2, 1, 1, 0), (3, 0, 1, 7), (4, 1, 0, 1), (5, 3, 0, 5)),
    ((0, 2, 0, 4), (1, 2, 0, 0), (2, 1, 1, 2), (3, 3, 1, 6), (4, 3, 0, 7), (5, 1, 0, 3)),
    ((0, 2, 1, 4), (1, 2, 0, 2), (2, 0, 1, 3), (3, 3, 1, 4), (4, 3, 1, 1), (5, 1, 1, 7)),
    ((0, 1, 0, 7), (1, 2, 0, 6), (2, 1, 1, 5), (3, 1, 1, 1), (4, 3, 0, 3), (5, 3, 1, 3)),
    ((0, 2, 1, 6), (1, 2, 1, 2), (2, 3, 1, 7), (3, 2, 1, 0), (4, 2, 0, 5), (5, 2, 0, 1)),
    ((0, 2, 1, 7), (1, 2, 0, 7), (2, 1, 1, 3), (3, 3, 1, 5), (4, 2, 0, 3), (5, 2, 1, 5)),
    ((0, 2, 1, 1), (1, 2, 1, 3)),
)
ENTRIES = tuple((t,) + e for t, row in enumerate(SCHEDULE) for e in row)
N_ENTRIES = len(ENTRIES)
GAP = 3
PIECE = 64
ORDER = (7, 8, 9, 10, 6, 5, 11, 12, 4, 3, 13, 14, 2, 1, 15)
Z_ORDER = (4, 3, 5, 2, 6, 1, 7, 0)
CHUNK = 4
GROUP = 256


def source_of(link, dx, dy, v):
    if link == 0:
        return (dx + 3) % 4, dy, v
    if link == 1:
        return (dx + 1) % 4, dy, v
    if link < 4:
        return dx, 1 - dy, v
    return dx, dy, v ^ 1


def group_plan():
    done = {}
    for t, _, dx, dy, v in ENTRIES:
        key = (dx, dy, v // 4)
        done[key] = max(done.get(key, 0), t)
    return done


GROUP_DONE = group_plan()
AHEAD = 1
LATE_FROM = len(SCHEDULE) - 1
LATE = tuple(key for key in GROUP_DONE if GROUP_DONE[key] >= LATE_FROM)
SPLIT = 6


def issue_plan():
    slot_of = {(dx, dy, v): t for t, _, dx, dy, v in ENTRIES}
    plan = [[] for _ in range(len(SCHEDULE) + GAP)]
    latest = {}
    for e, (t, link, dx, dy, v) in enumerate(ENTRIES):
        sx, sy, sv = source_of(link, dx, dy, v)
        have = 0 if (sx, sy) == (0, 0) else slot_of[sx, sy, sv] + GAP
        latest[link] = max(have, t - AHEAD, latest.get(link, 0))
        plan[latest[link]].append(e)
    return plan


ISSUE = issue_plan()


def lookup(index, values):
    out = jnp.int32(values[0])
    for i in range(1, len(values)):
        out = jnp.where(index == i, jnp.int32(values[i]), out)
    return out


def kernel(
    len_hbm, assign_hbm, adv_hbm, hid_ref, gain_hbm, w_ref, bias_hbm, ad_hbm, up_hbm, og_hbm,
    att_out, rec_c,
    len_ref, assign_ref, adv_ref, gain_ref, bias_ref, ad_ref, up_ref, og_ref,
    hbuf, nbuf, wbuf, wlate, acc, part_acc, ssq, kbuf, vbuf, low2, attb, pbuf, qg, lg,
    flags, pay_s, rec_s, ordered, pay_a, rec_a, pay_b, rec_b, pay_c,
    tokens, hsem, lsem, wsend, wrecv, psend, precv, msem, fsem, frecv, ssem, srecv, asem, arecv, bsem,
    brecv, gsem, grecv,
):
    me_d, me_f = lax.axis_index("dp"), lax.axis_index("fsdp")
    z, yh = me_d // 2, me_d % 2
    yl, x, c = me_f // 8, (me_f // 2) % 4, me_f % 2
    y = yh * 2 + yl
    par = z % 2
    chip = me_f // 2
    mate_f = me_f + 1 - 2 * c
    mate = (me_d, mate_f)

    def at(z_, y_, x_):
        return ((z_ % 8) * 2 + (y_ % 4) // 2, ((y_ % 4) % 2) * 8 + (x_ % 4) * 2 + c)

    receivers = (
        at(z, y, x + 3), at(z, y, x + 1), at(z, y + 3, x), at(z, y + 1, x), at(z + 7, y, x), at(z + 1, y, x),
    )
    neighbours = receivers + (mate,)
    y_pair, y_cross = y + 1 - 2 * yl, y - 1 + 2 * yl + 4
    f_peers = [(me_d, (me_f + k) % 16) for k in (4, 12, 5, 3, 11, 13, 2, 14, 6, 10, 7, 9, 8, 15, 1)]
    d_peers = [((me_d + k) % 16, me_f) for k in range(1, 16)]

    barrier = pltpu.get_barrier_semaphore()
    for peer in neighbours:
        pl.semaphore_signal(barrier, inc=1, device_id=peer, device_id_type=MESH)

    local = [
        pltpu.make_async_copy(src, dst, lsem.at[i])
        for i, (src, dst) in enumerate((
            (w_ref, wbuf.at[chip]), (ad_hbm, ad_ref), (og_hbm, og_ref), (len_hbm, len_ref), (assign_hbm, assign_ref),
            (adv_hbm, adv_ref), (gain_hbm, gain_ref), (bias_hbm, bias_ref), (up_hbm, up_ref),
        ))
    ]
    pl.semaphore_wait(barrier, 7)

    def hidden_copy(g):
        return pltpu.make_async_copy(
            hid_ref.at[:, pl.ds(pl.multiple_of(g * GROUP, GROUP), GROUP)], hbuf.at[g], hsem.at[g]
        )

    def start_hidden(g, carry):
        hidden_copy(g).start()
        return carry

    def send_tokens(i):
        for peer in neighbours:
            pl.semaphore_signal(tokens.at[i], inc=1, device_id=peer, device_id_type=MESH)

    def take_tokens(i):
        pl.semaphore_wait(tokens.at[i], 7)

    def shard(dx, dy):
        return (yl + dy - 2 * yl * dy) * 4 + (x + dx) % 4

    def rows_of(v):
        k = v + par if v % 2 == 0 else v - par
        return pl.ds(pl.multiple_of(k * PIECE, PIECE), PIECE)

    def piece_send(e):
        _, link, dx, dy, v = ENTRIES[e]
        sx, sy, sv = source_of(link, dx, dy, v)
        f, rows = shard(sx, sy), rows_of(sv)
        own = (sx, sy) == (0, 0)
        return pltpu.make_async_remote_copy(
            src_ref=w_ref.at[rows] if own else wbuf.at[f, rows],
            dst_ref=wbuf.at[f, rows],
            send_sem=wsend.at[e], recv_sem=wrecv.at[e],
            device_id=receivers[link], device_id_type=MESH,
        )

    def piece_landing(e):
        _, link, dx, dy, v = ENTRIES[e]
        spot = wbuf.at[shard(dx, dy), rows_of(v)]
        return pltpu.make_async_remote_copy(
            src_ref=spot, dst_ref=spot, send_sem=wsend.at[e], recv_sem=wrecv.at[e],
            device_id=mate, device_id_type=MESH,
        )

    def pass_on(i, v):
        dx, dy, h = LATE[i]
        k = v + par if v % 2 == 0 else v - par
        return pltpu.make_async_remote_copy(
            src_ref=wbuf.at[shard(dx, dy), rows_of(v)],
            dst_ref=wlate.at[i, pl.ds(pl.multiple_of((k - 4 * h) * PIECE, PIECE), PIECE)],
            send_sem=psend.at[4 * i + v - 4 * h], recv_sem=precv.at[4 * i + v - 4 * h],
            device_id=mate, device_id_type=MESH,
        )

    def multiply_late(i):
        dx, dy, h = LATE[i]
        g = (2 * shard(dx, dy) + 1 - c) * 2 + h
        acc[:256, :] += jnp.dot(nbuf[g, :256, :], wlate[i], preferred_element_type=jnp.float32)

    def multiply(items, rows):
        def body(i, carry):
            j = shard(lookup(i, [item[0] for item in items]), lookup(i, [item[1] for item in items]))
            h = lookup(i, [item[2] for item in items])
            span = pl.ds(pl.multiple_of(h * GROUP, GROUP), GROUP)
            acc[rows, :] += jnp.dot(
                nbuf[(2 * j + c) * 2 + h, rows, :], wbuf[j, span, :], preferred_element_type=jnp.float32
            )
            return carry

        lax.fori_loop(0, len(items), body, 0)

    def sum_squares(g, carry):
        hidden_copy(g).wait()
        wide = hbuf[g].astype(jnp.float32)
        squared = wide * wide
        ssq[...] += squared[:, :128] + squared[:, 128:]
        return carry

    def scale_group(g, carry):
        gain = gain_ref[:, pl.ds(pl.multiple_of(g * GROUP, GROUP), GROUP)]
        nbuf[g, :256, :] = (hbuf[g].astype(jnp.float32) * ssq[:, :1] * gain).astype(jnp.bfloat16)
        return carry

    def lora_group(g, carry):
        cols = pl.ds(pl.multiple_of(g * GROUP, GROUP), GROUP)
        low2[...] += lax.dot_general(nbuf[g, :256, :], ad_ref[:, cols], NT, preferred_element_type=jnp.float32)
        return carry

    flag_copies = [
        pltpu.make_async_remote_copy(
            src_ref=flags.at[me_d], dst_ref=flags.at[me_d], send_sem=fsem.at[k], recv_sem=frecv.at[k],
            device_id=d_peers[k], device_id_type=MESH,
        )
        for k in range(15)
    ]
    def norm_copy(i):
        if i < 8:
            place = pl.ds((2 * i + 1 - c) * 2, 2)
        else:
            place = pl.ds((2 * (i - 8) + c) * 2 + 1 - c, 1)
        return pltpu.make_async_remote_copy(
            src_ref=nbuf.at[place, pl.ds(0, 256)], dst_ref=nbuf.at[place, pl.ds(256, 256)],
            send_sem=msem.at[0, i], recv_sem=msem.at[1, i], device_id=mate, device_id_type=MESH,
        )

    def part_copy(half):
        rows = pl.ds(half * 128, 128)
        return pltpu.make_async_remote_copy(
            src_ref=acc.at[pl.ds(256 + half * 128, 128)], dst_ref=part_acc.at[rows],
            send_sem=msem.at[0, 17 + half], recv_sem=msem.at[1, 17 + half], device_id=mate, device_id_type=MESH,
        )

    row = lax.broadcasted_iota(jnp.int32, (128, 128), 0)
    col = lax.broadcasted_iota(jnp.int32, (128, 128), 1)
    same = (row // 32) == (col // 32)
    causal = same & ((col % 32) <= (row % 32))
    scale = 128 ** (-0.5)
    heads = [slice(h * 128, h * 128 + 128) for h in range(4)]

    def spread(ref, half, where, kind):
        out = jnp.full((128, 128), ref[half * 4].astype(kind), kind)
        for r in range(1, 4):
            out = jnp.where(where // 32 == r, jnp.full((128, 128), ref[half * 4 + r].astype(kind), kind), out)
        return out

    by_step = [[e for e in range(N_ENTRIES) if ENTRIES[e][0] == t] for t in range(len(SCHEDULE))]
    ready = [(0, 0, 0), (0, 0, 1)]
    mine, others = slice(0, 256), slice(256, 512)
    n_steps = len(SCHEDULE) + GAP
    for t in range(n_steps):
        if t >= GAP:
            for e in by_step[t - GAP]:
                piece_landing(e).wait_recv()
                _, _, dx, dy, v = ENTRIES[e]
                if (dx, dy, v // 4) in LATE:
                    pass_on(LATE.index((dx, dy, v // 4)), v).start()
        for e in ISSUE[t]:
            piece_send(e).start()
        if 1 <= t <= 5:
            take_tokens(t - 1)
        if t < 5:
            send_tokens(t)
        for key, done in GROUP_DONE.items():
            if done == t - GAP and key not in LATE:
                ready.append(key)
        if t == 0:
            lax.fori_loop(0, 32, start_hidden, 0)
            for copy in local:
                copy.start()
            ssq[...] = jnp.zeros_like(ssq)
            low2[...] = jnp.zeros_like(low2)
            lax.fori_loop(0, 16, sum_squares, 0)
        if t == 1:
            lax.fori_loop(16, 32, sum_squares, 0)
            mean = jnp.sum(ssq[...], axis=1, keepdims=True) * (1.0 / 8192.0)
            ssq[...] = jnp.broadcast_to(lax.rsqrt(mean + EPSILON), ssq.shape)
            local[6].wait()
        if t == 2:
            lax.fori_loop(0, 16, scale_group, 0)
            for i in (0, 1, 2, 3, 8, 9, 10, 11):
                norm_copy(i).start()
        if t == 3:
            lax.fori_loop(16, 32, scale_group, 0)
            for i in (4, 5, 6, 7, 12, 13, 14, 15):
                norm_copy(i).start()
            local[1].wait()
        if t == 4:
            lax.fori_loop(0, 16, lora_group, 0)
        if t == 5:
            lax.fori_loop(16, 32, lora_group, 0)
            local[0].wait()
            local[7].wait()
            acc[mine, :] = jnp.broadcast_to(bias_ref[...].astype(jnp.float32).reshape(1, 768), (256, 768))
            acc[others, :] = jnp.zeros((256, 768), jnp.float32)
            for i in range(16):
                norm_copy(i).wait_recv()
        if t == 6:
            for i in (2, 3, 4, 5, 8):
                local[i].wait()
            lora = jnp.dot(low2[...].astype(jnp.bfloat16), up_ref[...], preferred_element_type=jnp.float32)
            acc[mine, :512] += ADAPTER_SCALE * lora
            for half in range(2):
                rows = slice(half * 128, half * 128 + 128)
                factor = spread(adv_ref, half, row, jnp.float32) / spread(len_ref, half, row, jnp.float32)
                live = (row % 32) < spread(len_ref, half, row, jnp.int32)
                for h in heads:
                    weighted = (og_ref[rows, h].astype(jnp.float32) * factor).astype(jnp.bfloat16)
                    og_ref[rows, h] = jnp.where(live, weighted.astype(jnp.float32), 0.0).astype(jnp.bfloat16)
            for r in range(8):
                flags[me_d, pl.ds(r, 1), :] = jnp.full((1, 128), assign_ref[r], jnp.int32)
            for copy in flag_copies:
                copy.start()
        if t >= 6 and ready:
            multiply(ready, slice(0, 512))
            ready = []
        if t == LATE_FROM - 1 + GAP:
            part_copy(0).start()
            part_copy(1).start()
    multiply(LATE, mine)
    for i in range(len(LATE)):
        for v in range(4 * LATE[i][2], 4 * LATE[i][2] + 4):
            pass_on(i, v).wait_recv()
        multiply_late(i)

    low = low2[...].astype(jnp.bfloat16)
    low_wide = jnp.concatenate([low, low], axis=1)
    lives = [(row % 32) < spread(len_ref, half, row, jnp.int32) for half in range(2)]
    seen = [causal & ((col % 32) < spread(len_ref, half, col, jnp.int32)) for half in range(2)]
    for half in range(2):
        rows = slice(half * 128, half * 128 + 128)
        part_copy(half).wait_recv()
        projected = acc[rows, :] + part_acc[rows, :]
        queries = projected[:, :512].astype(jnp.bfloat16)
        keys = projected[:, 512:640].astype(jnp.bfloat16)
        values = projected[:, 640:].astype(jnp.bfloat16)
        kbuf[rows, :] = keys
        vbuf[rows, :] = values
        scores = [lax.dot_general(queries[:, h], keys, NT, preferred_element_type=jnp.float32) for h in heads]
        scores = [jnp.where(seen[half], s * scale, jnp.float32(-1e30)) for s in scores]
        raised = [jnp.exp(s - jnp.max(s, axis=-1, keepdims=True)) for s in scores]
        soft = [r / jnp.sum(r, axis=-1, keepdims=True) for r in raised]
        outs = [jnp.dot(p.astype(jnp.bfloat16), values, preferred_element_type=jnp.float32) for p in soft]
        for i, h in enumerate(heads):
            pbuf[half * 4 + i] = soft[i]
            out = jnp.where(lives[half], outs[i], 0.0).astype(jnp.bfloat16)
            attb[half * 4 : half * 4 + 4, :, h] = out.reshape(4, 32, 128)

    for half in range(2):
        rows = slice(half * 128, half * 128 + 128)
        keys, values = kbuf[rows, :], vbuf[rows, :]
        weighted = [og_ref[rows, h] for h in heads]
        dsoft = [lax.dot_general(w, values, NT, preferred_element_type=jnp.float32) for w in weighted]
        dsoft = [d.astype(jnp.bfloat16).astype(jnp.float32) for d in dsoft]
        soft = [pbuf[half * 4 + i] for i in range(4)]
        inner = [jnp.sum(d * p, axis=-1, keepdims=True) for d, p in zip(dsoft, soft)]
        dscores = [(p * (d - i) * scale).astype(jnp.bfloat16) for d, p, i in zip(dsoft, soft, inner)]
        dquery = [jnp.dot(d, keys, preferred_element_type=jnp.float32) for d in dscores]
        for d, h in zip(dquery, heads):
            qg[rows, h] = d.astype(jnp.bfloat16)
    low_grad = ADAPTER_SCALE * lax.dot_general(up_ref[...], qg[...], NT, preferred_element_type=jnp.float32)
    lg[:, :256] = low_grad.astype(jnp.bfloat16)
    lg_copy = pltpu.make_async_remote_copy(
        src_ref=lg.at[:, pl.ds(0, 256)], dst_ref=lg.at[:, pl.ds(256, 256)], send_sem=msem.at[0, 16], recv_sem=msem.at[1, 16],
        device_id=mate, device_id_type=MESH,
    )
    lg_copy.start()
    up_grad = ADAPTER_SCALE * lax.dot_general(qg[...], low_wide, TN, preferred_element_type=jnp.float32)
    up_four = up_grad.reshape(16, 2, 16, 128)
    lane = lax.broadcasted_iota(jnp.int32, (16, 16, 128), 2)
    ordered[...] = jnp.where(lane < 64, up_four[:, 0], up_four[:, 1]).astype(jnp.bfloat16)
    def fill_slot(d, carry):
        which = jnp.int32(0)
        for r in range(1, 8):
            which = jnp.where(assign_ref[r] == d, jnp.int32(r), which)
        pay_s[d] = attb[which]
        return carry

    lax.fori_loop(0, 16, fill_slot, 0)
    rec_s[me_d] = pay_s[me_d]
    slot_copies = [
        pltpu.make_async_remote_copy(
            src_ref=pay_s.at[(me_d + ORDER[i]) % 16], dst_ref=rec_s.at[me_d], send_sem=ssem.at[i],
            recv_sem=srecv.at[i], device_id=((me_d + ORDER[i]) % 16, me_f), device_id_type=MESH,
        )
        for i in range(15)
    ]
    for copy in slot_copies[:SPLIT]:
        copy.start()
    lg_copy.wait()

    def down_slice(i, carry):
        d = (z + lookup(i // 2, Z_ORDER)) % 8 * 2 + i % 2
        part = jnp.dot(lg[...], nbuf[2 * d + c], preferred_element_type=jnp.float32).astype(jnp.bfloat16)
        for i2 in range(4):
            for j2 in range(2):
                pay_a[j2 * 4 + i2, i] = part[i2 * 16 : i2 * 16 + 16, j2 * 128 : j2 * 128 + 128]
        return carry

    def a_copy(q, k):
        span = pl.ds(q * CHUNK, CHUNK)
        there = (chip + k) % 8
        other = (there // 4 + yl) % 2
        y_to = y + other * ((y_cross if q % 2 else y_pair) - y)
        return pltpu.make_async_remote_copy(
            src_ref=pay_a.at[there, span], dst_ref=rec_a.at[k - 1, span], send_sem=asem.at[q, k - 1],
            recv_sem=arecv.at[q], device_id=at(z, y_to, there % 4), device_id_type=MESH,
        )

    chunks = range(16 // CHUNK)
    for q in chunks:
        lax.fori_loop(q * CHUNK, (q + 1) * CHUNK, down_slice, 0)
        for k in range(1, 8):
            a_copy(q, k).start()
    def slice_at(i):
        return (z + Z_ORDER[i // 2]) % 8 * 2 + i % 2

    def b_copy(i):
        slot = i - i % 2 + yh if i < 14 else 14
        return pltpu.make_async_remote_copy(
            src_ref=pay_b.at[i if i < 14 else 15 - yh], dst_ref=rec_b.at[slot], send_sem=bsem.at[i],
            recv_sem=brecv.at[0], device_id=(slice_at(i) if i < 14 else 2 * z + 1 - yh, me_f), device_id_type=MESH,
        )

    for q in chunks:
        span = pl.ds(q * CHUNK, CHUNK)
        arrived = rec_a.at[:, span]
        pltpu.make_async_copy(arrived, arrived, arecv.at[q]).wait()
        total = pay_a[chip, span].astype(jnp.float32)
        for k in range(7):
            total += rec_a[k, span].astype(jnp.float32)
        pay_b[span, 0] = total.astype(jnp.bfloat16)
        for i in range(q * CHUNK, (q + 1) * CHUNK):
            pay_b[i, 1] = ordered[slice_at(i)]
            if i < 14:
                b_copy(i).start()
    b_copy(14).start()

    for copy in slot_copies[SPLIT:]:
        copy.start()
    for e in range(N_ENTRIES):
        piece_send(e).wait_send()
    for i in range(16):
        norm_copy(i).wait_send()
    for half in range(2):
        part_copy(half).wait_send()
    for i in range(len(LATE)):
        for v in range(4 * LATE[i][2], 4 * LATE[i][2] + 4):
            pass_on(i, v).wait_send()
    for copy in flag_copies:
        copy.wait()
    for q in chunks:
        for k in range(1, 8):
            a_copy(q, k).wait_send()
    pltpu.make_async_copy(rec_b, rec_b, brecv.at[0]).wait()
    total = pay_b[14 + yh].astype(jnp.float32)
    for k in range(15):
        total += rec_b[k].astype(jnp.float32)
    pay_c[...] = total.astype(jnp.bfloat16)
    c_copies = [
        pltpu.make_async_remote_copy(
            src_ref=pay_c, dst_ref=rec_c.at[me_f], send_sem=gsem.at[0], recv_sem=grecv.at[0],
            device_id=f_peers[k], device_id_type=MESH,
        )
        for k in range(15)
    ]
    for copy in c_copies:
        copy.start()
    own_copy = pltpu.make_async_copy(pay_c, rec_c.at[me_f], lsem.at[10])
    own_copy.start()
    for copy in slot_copies:
        copy.wait()
    held = [jnp.sum((flags[s] == me_d).astype(jnp.float32), axis=0, keepdims=True) for s in range(16)]
    before = [jnp.zeros((1, 128), jnp.float32)]
    for s in range(15):
        before.append(before[-1] + held[s])
    for i in range(8):
        picked = jnp.zeros((32, 512), jnp.bfloat16)
        for s in range(i, i + 9):
            take = jnp.where(before[s] == float(i), held[s], 0.0).astype(jnp.bfloat16)
            picked += rec_s[s] * jnp.concatenate([take] * 4, axis=1)
        attb[i] = picked
    att_copy = pltpu.make_async_copy(attb, att_out, lsem.at[9])
    att_copy.start()

    for i in range(15):
        b_copy(i).wait_send()
    most = rec_c.at[pl.ds(0, 15)]
    pltpu.make_async_copy(most, most, grecv.at[0]).wait()
    pltpu.make_async_copy(most, most, gsem.at[0]).wait()
    own_copy.wait()
    att_copy.wait()


def assemble(att_ref, sums_ref, att_out, down_out, up_out):
    att_out[...] = att_ref[...]
    for f in range(16):
        j, i, core = f // 8, (f // 2) % 4, f % 2
        down_out[i * 16 : i * 16 + 16, core * 256 + j * 128 : core * 256 + j * 128 + 128] = sums_ref[f, 0].astype(
            jnp.float32
        )
    total = sums_ref[0, 1].astype(jnp.float32)
    for f in range(1, 16):
        total += sums_ref[f, 1].astype(jnp.float32)
    up_out[:16, :] = total[:, :64]
    up_out[16:, :] = total[:, 64:]


def on_device(
    hidden_input, input_norm_gain, joined_weight, joined_bias, adapter_down, adapter_up, advantage,
    output_gradient, lengths, assignment,
):
    bf16, f32 = jnp.bfloat16, jnp.float32
    dma = pltpu.SemaphoreType.DMA
    vmem = pl.BlockSpec(memory_space=pltpu.VMEM)
    hbm = pl.BlockSpec(memory_space=pl.ANY)
    att, sums = pl.pallas_call(
        kernel,
        out_shape=(jax.ShapeDtypeStruct((8, 32, 512), bf16), jax.ShapeDtypeStruct((16, 2, 16, 128), bf16)),
        in_specs=[hbm] * 10,
        out_specs=(hbm, hbm),
        scratch_shapes=[
            pltpu.SMEM((8,), jnp.int32),
            pltpu.SMEM((8,), jnp.int32),
            pltpu.SMEM((8,), f32),
            pltpu.VMEM((1, 8192), f32),
            pltpu.VMEM((768,), bf16),
            pltpu.VMEM((64, 8192), bf16),
            pltpu.VMEM((64, 512), bf16),
            pltpu.VMEM((256, 512), bf16),
            pltpu.VMEM((32, 256, 256), bf16),
            pltpu.VMEM((32, 512, 256), bf16),
            pltpu.VMEM((8, 512, 768), bf16),
            pltpu.VMEM((len(LATE), 256, 768), bf16),
            pltpu.VMEM((512, 768), f32),
            pltpu.VMEM((256, 768), f32),
            pltpu.VMEM((256, 128), f32),
            pltpu.VMEM((256, 128), bf16),
            pltpu.VMEM((256, 128), bf16),
            pltpu.VMEM((256, 64), f32),
            pltpu.VMEM((8, 32, 512), bf16),
            pltpu.VMEM((8, 128, 128), f32),
            pltpu.VMEM((256, 512), bf16),
            pltpu.VMEM((64, 512), bf16),
            pltpu.VMEM((16, 8, 128), jnp.int32),
            pltpu.VMEM((16, 32, 512), bf16),
            pltpu.VMEM((16, 32, 512), bf16),
            pltpu.VMEM((16, 16, 128), bf16),
            pltpu.VMEM((8, 16, 16, 128), bf16),
            pltpu.VMEM((7, 16, 16, 128), bf16),
            pltpu.VMEM((16, 2, 16, 128), bf16),
            pltpu.VMEM((15, 2, 16, 128), bf16),
            pltpu.VMEM((2, 16, 128), bf16),
            pltpu.SemaphoreType.REGULAR((5,)),
            dma((32,)), dma((11,)), dma((N_ENTRIES,)), dma((N_ENTRIES,)), dma((4 * len(LATE),)), dma((4 * len(LATE),)),
            dma((2, 19)), dma((15,)), dma((15,)), dma((15,)), dma((15,)), dma((16 // CHUNK, 7)), dma((16 // CHUNK,)),
            dma((15,)), dma((1,)), dma((1,)), dma((1,)),
        ],
        compiler_params=pltpu.CompilerParams(
            collective_id=0, has_side_effects=True, vmem_limit_bytes=56 * 2**20
        ),
        name="block",
    )(
        lengths,
        assignment,
        advantage,
        hidden_input.reshape(256, 8192),
        input_norm_gain.reshape(1, 8192),
        joined_weight,
        joined_bias,
        adapter_down.T,
        adapter_up,
        output_gradient.reshape(256, 512),
    )
    att, down, up = pl.pallas_call(
        assemble,
        out_shape=(
            jax.ShapeDtypeStruct((8, 32, 512), bf16),
            jax.ShapeDtypeStruct((64, 512), f32),
            jax.ShapeDtypeStruct((32, 64), f32),
        ),
        in_specs=[vmem, vmem],
        out_specs=(vmem, vmem, vmem),
        name="assemble",
    )(att, sums)
    return att, down.T, up.T


def solution(mesh):
    in_specs = (
        P(("dp", "fsdp"), None, None),
        P(),
        P("fsdp", None),
        P(),
        P(),
        P(),
        P(("dp", "fsdp")),
        P(("dp", "fsdp"), None, None),
        P(("dp", "fsdp")),
        P(("dp", "fsdp")),
    )
    out_specs = (P(("dp", "fsdp"), None, None), P("dp", None), P(None, "dp"))
    return jax.shard_map(
        on_device, mesh=mesh, in_specs=in_specs, out_specs=out_specs, check_vma=False
    )
```
